32 devices in a mesh: groups: 1, res: 16 (over z, y, core), sub: 2 (over x).
Axes of the slice: x: 2, y: 2, z: 4, core: 2. Of those that a mesh axis runs over, the one named last changes fastest.
Arguments:
- sequence_embedding: bfloat16 [16, 256, 64], P('sub', ('groups', 'res')), may hold values from -6 to 6
- sequence_present_flags: int32 [16, 256], P('sub', ('groups', 'res')), may hold values 0 or 1
- position_couple_flags: int32 [256, 256], P(('groups', 'res'), 'sub'), may hold values 0 or 1
- first_factor_matrix: bfloat16 [64, 32], replicated, may hold values from -0.75 to 0.75
- second_factor_matrix: bfloat16 [64, 32], replicated, may hold values from -0.75 to 0.75
- final_linear_matrix: bfloat16 [1024, 128], replicated, may hold values from -0.1875 to 0.1875
- final_offset_vector: float32 [128], replicated, may hold values from -3 to 3
- couple_change_cotangent: float32 [256, 256, 128], P(('groups', 'res'), 'sub'), may hold values from -6 to 6
Outputs:
- pair_delta_output: bfloat16 [256, 256, 128], P(('groups', 'res'), 'sub')
- alignment_gradient: float32 [16, 256, 64], P('sub', ('groups', 'res'))
- left_weight_gradient: float32 [64, 32], P('groups')
- right_weight_gradient: float32 [64, 32], P('groups')
- output_weight_gradient: float32 [1024, 128], P('groups')
- output_bias_gradient: float32 [128], P('groups')
The draws below stay inside these ranges and needn't reach their ends.
All inputs are finite; a program needn't handle non-finite values. No bound on the sum of `sequence_present_flags` or of `position_couple_flags` on one device may be relied on, other than what follows from the above.
Results may differ from the reference program's by a relative error of at most 0.0074.
Values may be sent and summed in bfloat16 or wider, within the bound.
A program may use at most 64 MiB of HBM per device.

```python
import jax
import jax.numpy as jnp
from jax import lax

FEATURE_COUNT = 64
FACTOR_DEPTH = 32
CZ = 128
SEQUENCE_COUNT = 16
POSITION_COUNT = 256


def with_ends(entries, key, least, top_value):
    longest = entries.shape.index(max(entries.shape))
    spots = []
    for shift in (0, 1):
        where = [jax.random.randint(jax.random.fold_in(key, axis), (), 0, length) for axis, length in enumerate(entries.shape)]
        where[longest] = (where[longest] + shift) % entries.shape[longest]
        spots.append(tuple(where))
    return entries.at[spots[0]].set(least).at[spots[1]].set(top_value)


def spiked(drawn, key, source, target, parts, factor):
    def block_of(dim):
        return (jnp.arange(drawn.shape[dim]) // (drawn.shape[dim] // parts)).reshape((-1,) + (1,) * (drawn.ndim - 1 - dim))

    one_side = jax.random.permutation(key, parts)[block_of(target)]
    second = (block_of(target) + parts // 2) % parts
    return jnp.where((block_of(source) == one_side) | (block_of(source) == second), factor * drawn, drawn)


def level_of(stream_key, extent, cuts, low, top_value):
    def one(position, parts):
        steps = jax.random.uniform(jax.random.fold_in(jax.random.fold_in(stream_key, 6), position), (parts,), jnp.float32, low / len(cuts), top_value / len(cuts))
        return jnp.repeat(jnp.exp(steps), extent[position] // parts).reshape((-1,) + (1,) * (len(extent) - position - 1))

    factor_of = one(*cuts[0])
    for cut in cuts[1:]:
        factor_of = factor_of * one(*cut)
    return factor_of


def scatter_about(key, dims, deviation, limit, pieces=(), dtype=jnp.bfloat16):
    array = deviation * jax.random.normal(key, dims, jnp.float32)
    if pieces:
        array = array * level_of(key, dims, pieces, -0.22, 0.18)
    return jnp.clip(array, -limit, limit).astype(dtype)


def bell_draw_with(rng, shape, deviation, most, shards, heavy, held_as=jnp.bfloat16):
    array = deviation * jax.random.normal(rng, shape, jnp.float32)
    if shards:
        array = array * level_of(rng, shape, shards, -0.22, 0.18)
    return jnp.clip(spiked(array, jax.random.fold_in(rng, 3), *heavy), -most, most).astype(held_as)


def setup_inputs(seed: int = 0, part: int = 0) -> dict:
    keys = jax.random.split(jax.random.key(seed), 9)
    part_keys = jax.random.split(jax.random.fold_in(keys[8], part), 9)
    sequence_embedding = scatter_about(part_keys[0], (SEQUENCE_COUNT, POSITION_COUNT, FEATURE_COUNT), 1.0, 6.0, ((0, 2), (1, 16)))
    sequence_present_flags = with_ends((jax.random.randint(part_keys[1], (SEQUENCE_COUNT, POSITION_COUNT), 0, 2) < 1).astype(jnp.int32), jax.random.fold_in(part_keys[1], 1), 0, 1)
    position_couple_flags = with_ends((jax.random.randint(part_keys[2], (POSITION_COUNT, POSITION_COUNT), 0, 4) < 3).astype(jnp.int32), jax.random.fold_in(part_keys[2], 1), 0, 1)
    first_factor_matrix = scatter_about(keys[3], (FEATURE_COUNT, FACTOR_DEPTH), FEATURE_COUNT ** -0.5, 0.75)
    second_factor_matrix = scatter_about(keys[4], (FEATURE_COUNT, FACTOR_DEPTH), FEATURE_COUNT ** -0.5, 0.75)
    final_linear_matrix = scatter_about(keys[5], (FACTOR_DEPTH * FACTOR_DEPTH, CZ), (FACTOR_DEPTH * FACTOR_DEPTH) ** -0.5, 0.1875)
    final_offset_vector = scatter_about(keys[6], (CZ,), 0.5, 3.0, (), jnp.float32)
    couple_change_cotangent = bell_draw_with(part_keys[7], (POSITION_COUNT, POSITION_COUNT, CZ), 1.0, 6.0, ((0, 16), (1, 2)), (0, 1, 16, 2.0), jnp.float32)
    return {"sequence_embedding": sequence_embedding, "sequence_present_flags": sequence_present_flags, "position_couple_flags": position_couple_flags, "first_factor_matrix": first_factor_matrix, "second_factor_matrix": second_factor_matrix, "final_linear_matrix": final_linear_matrix, "final_offset_vector": final_offset_vector, "couple_change_cotangent": couple_change_cotangent}


def reference(sequence_embedding, sequence_present_flags, position_couple_flags, first_factor_matrix, second_factor_matrix, final_linear_matrix, final_offset_vector, couple_change_cotangent):
    highest = lax.Precision.HIGHEST
    precise_scalar = jnp.float32
    present_count_items = sequence_embedding.astype(precise_scalar)
    centred = present_count_items - lax.optimization_barrier(jnp.mean(present_count_items, axis=-1, keepdims=True))
    variance = lax.optimization_barrier(jnp.mean(centred * centred, axis=-1, keepdims=True))
    reciprocal_deviation = lax.rsqrt(variance + 1e-05)
    normalized_input = centred * reciprocal_deviation
    layer_scaled_half = normalized_input.astype(jnp.bfloat16)
    row_presence_mask = sequence_present_flags.astype(precise_scalar)[..., None]
    layer_scaled_flat = layer_scaled_half.reshape(SEQUENCE_COUNT * POSITION_COUNT, FEATURE_COUNT)
    first_factor_features = jnp.dot(layer_scaled_flat, first_factor_matrix, preferred_element_type=precise_scalar).reshape(SEQUENCE_COUNT, POSITION_COUNT, FACTOR_DEPTH)
    second_factor_features = jnp.dot(layer_scaled_flat, second_factor_matrix, preferred_element_type=precise_scalar).reshape(SEQUENCE_COUNT, POSITION_COUNT, FACTOR_DEPTH)
    feat_a = (first_factor_features * row_presence_mask).astype(jnp.bfloat16)
    feat_b = (second_factor_features * row_presence_mask).astype(jnp.bfloat16)
    float_mask = sequence_present_flags.astype(precise_scalar)
    divisor = jnp.maximum(jnp.einsum('si,sj->ij', float_mask, float_mask), 1.0)[..., None]
    out_cube = final_linear_matrix.astype(precise_scalar).reshape(FACTOR_DEPTH, FACTOR_DEPTH, CZ)
    tmix = jnp.einsum('sic,cde->side', feat_a.astype(precise_scalar), out_cube).astype(jnp.bfloat16)
    zsum = jnp.einsum('side,sjd->ije', tmix.astype(precise_scalar), feat_b.astype(precise_scalar))
    pmask = position_couple_flags.astype(precise_scalar)[..., None]
    pair_delta_output = (pmask * (zsum + final_offset_vector) / divisor).astype(jnp.bfloat16)
    gscaled32 = couple_change_cotangent * pmask / divisor
    output_bias_gradient = lax.optimization_barrier(jnp.sum(gscaled32, axis=(0, 1))) / POSITION_COUNT
    gscaled = gscaled32.astype(jnp.bfloat16).astype(precise_scalar)
    dtmix = jnp.einsum('ije,sjd->side', gscaled, feat_b.astype(precise_scalar))
    dfeat_b = jnp.einsum('ije,side->sjd', gscaled, tmix.astype(precise_scalar)) * row_presence_mask
    dfeat_a = jnp.einsum('side,cde->sic', dtmix, out_cube, precision=highest) * row_presence_mask
    output_weight_gradient = jnp.einsum('sic,side->cde', feat_a.astype(precise_scalar), dtmix, precision=highest).reshape(FACTOR_DEPTH * FACTOR_DEPTH, CZ) / POSITION_COUNT
    normed_f = layer_scaled_half.astype(precise_scalar)
    left_weight_gradient = jnp.einsum('sim,sic->mc', normed_f, dfeat_a, precision=highest) / POSITION_COUNT
    right_weight_gradient = jnp.einsum('sim,sic->mc', normed_f, dfeat_b, precision=highest) / POSITION_COUNT
    normalized_gradient = jnp.einsum('sic,mc->sim', dfeat_a, first_factor_matrix.astype(precise_scalar), precision=highest)
    normalized_gradient = normalized_gradient + jnp.einsum('sic,mc->sim', dfeat_b, second_factor_matrix.astype(precise_scalar), precision=highest)
    alignment_gradient = reciprocal_deviation * (normalized_gradient - lax.optimization_barrier(jnp.mean(normalized_gradient, axis=-1, keepdims=True)) - normalized_input * lax.optimization_barrier(jnp.mean(normalized_gradient * normalized_input, axis=-1, keepdims=True)))
    return (pair_delta_output, alignment_gradient, left_weight_gradient, right_weight_gradient, output_weight_gradient, output_bias_gradient)
```

```python
import functools

import jax
import jax.numpy as jnp
from jax import lax
from jax.sharding import PartitionSpec as P
from jax.experimental import pallas as pl
from jax.experimental.pallas import tpu as pltpu


MESH = pl.DeviceIdType.MESH


def onehot(shape, test):
    rows = lax.broadcasted_iota(jnp.int32, shape, 0)
    lanes = lax.broadcasted_iota(jnp.int32, shape, 1)
    return jnp.where(test(rows, lanes), 1.0, 0.0)


def dot(a, b, dims=((1,), (0,)), precision=None):
    return lax.dot_general(a, b, (dims, ((), ())), preferred_element_type=jnp.float32, precision=precision)


def kernel(
    nres, nsub,
    emb, flags, pflags, wab, lin, offset, cot_hbm,
    pair, align, wa_out, wb_out, lin_out, bias_out,
    cot, feat, other, blk, bmat, wm, lin32, tmat, gmat, dmat, wide, dstage, drecv,
    ostage, orecv, ogather, da_send, da_recv, small, small_recv, rows_out,
    cot_sem, bsend, brecv, dsend, drecv_sem, osend, orecv_sem, gsend, grecv, wsend, wrecv, psend, precv,
):
    bf16, f32 = jnp.bfloat16, jnp.float32
    n = nres * nsub
    nblk = nres // nsub
    r, u = lax.axis_index("res"), lax.axis_index("sub")
    me = r * nsub + u

    def place(k):
        return {"res": k // nsub, "sub": lax.rem(k, nsub)}

    cot_copy = pltpu.make_async_copy(cot_hbm, cot, cot_sem)
    cot_copy.start()
    barrier = pltpu.get_barrier_semaphore()

    def greet(k, carry):
        pl.semaphore_signal(barrier, inc=1, device_id=place(lax.rem(me + k, n)), device_id_type=MESH)
        return carry

    lax.fori_loop(1, n, greet, 0)

    x = dot(onehot((128, 128), lambda a, b: b == (a % 8) * 16 + a // 8).astype(bf16), emb[...].reshape(128, 64))
    centred = x - jnp.mean(x, axis=-1, keepdims=True)
    inv_std = lax.rsqrt(jnp.mean(centred * centred, axis=-1, keepdims=True) + 1e-05)
    normed = centred * inv_std
    normed16 = normed.astype(bf16)
    picked = dot(onehot((128, 8), lambda a, b: a % 8 == b).astype(bf16), flags[...].astype(f32).astype(bf16))
    mask = jnp.sum(picked * onehot((128, 16), lambda a, b: a // 8 == b), axis=1, keepdims=True)
    projected = dot(normed16, wab[...]) * mask
    projected = projected + mask * onehot((128, 128), lambda a, b: b - 64 == a % 8)
    feat[...] = projected.astype(bf16)
    keep = onehot((128, 384), lambda a, b: a % 8 == b % 8)
    spread = onehot((128, 384), lambda a, b: ((b < 256) & (a == 32 + b // 8)) | ((a >= 64) & (b - 256 == a)))
    gather_rows = onehot((16, 128), lambda a, b: a == b // 8).astype(bf16)
    mine = dot(gather_rows, (dot(feat[...], spread.astype(bf16)) * keep).astype(bf16)).astype(bf16)
    blk[...] = mine
    home = r // nblk
    slot = u * nblk + lax.rem(r, nblk)
    rows_here = pl.ds(pl.multiple_of(lax.rem(r, nblk) * 16, 16), 16)

    pl.semaphore_wait(barrier, n - 1)

    def partner_copy():
        return pltpu.make_async_remote_copy(
            src_ref=feat, dst_ref=other, send_sem=psend.at[0], recv_sem=precv.at[0],
            device_id={"res": r, "sub": 1 - u}, device_id_type=MESH)

    partner_copy().start()

    def block_copy(k):
        q = lax.rem(r + k, nres)
        return pltpu.make_async_remote_copy(
            src_ref=blk, dst_ref=bmat.at[u, rows_here, :], send_sem=bsend.at[k], recv_sem=brecv.at[slot],
            device_id={"res": q, "sub": home}, device_id_type=MESH)

    def send_block(k, carry):
        block_copy(k).start()
        return carry

    lax.fori_loop(1, nres, send_block, 0)

    @pl.when(home != u)
    def _():
        block_copy(0).start()

    @pl.when(home == u)
    def _():
        bmat[u, rows_here, :] = mine

    lin32[...] = lin[...].astype(f32)
    wm[...] = jnp.zeros_like(wm)
    for d in range(32):
        piece = lin32[pl.ds(d, 32, stride=32), :].astype(bf16)
        wm[0:32, d * 128:(d + 1) * 128] = piece
        wm[64:96, d * 128:(d + 1) * 128] = piece

    lane128 = lax.broadcasted_iota(jnp.int32, (128, 128), 1)

    def left_only(ref):
        return jnp.where(lane128 < 32, ref[...].astype(f32), 0.0)

    def mix(half, left):
        def step(p, carry):
            part = dot(left, wm[:, pl.ds(pl.multiple_of(p * 256, 256), 256)])
            for i in range(16):
                rows = part[i * 8:(i + 1) * 8, :]
                pair_rows = jnp.concatenate([rows[:, :128], rows[:, 128:]], axis=0)
                tmat[half, pl.ds(pl.multiple_of(p * 16, 16), 16), i * 128:(i + 1) * 128] = pair_rows.astype(bf16)
            return carry

        lax.fori_loop(0, 16, step, 0)

    mine_left = left_only(feat)
    mix(u, mine_left.astype(bf16))
    partner_copy().wait()
    other_left = left_only(other)
    mix(1 - u, other_left.astype(bf16))

    mask_rows = [dot(gather_rows, ref[...]).astype(bf16) for ref in (feat, other)]

    cot_copy.wait()

    def wait_block(k, carry):
        @pl.when(k != slot)
        def _():
            copy = pltpu.make_async_remote_copy(
                src_ref=blk, dst_ref=bmat.at[k // nblk, pl.ds(pl.multiple_of(lax.rem(k, nblk) * 16, 16), 16), :],
                send_sem=bsend.at[0], recv_sem=brecv.at[k], device_id={"res": r, "sub": 1 - u}, device_id_type=MESH)
            copy.wait_recv()

        @pl.when((k == slot) & (home != u))
        def _():
            copy = pltpu.make_async_remote_copy(
                src_ref=blk, dst_ref=bmat.at[k // nblk, pl.ds(pl.multiple_of(lax.rem(k, nblk) * 16, 16), 16), :],
                send_sem=bsend.at[0], recv_sem=brecv.at[k], device_id={"res": r, "sub": 1 - u}, device_id_type=MESH)
            copy.wait_recv()

        return carry

    lax.fori_loop(0, nres, wait_block, 0)

    count = dot(mask_rows[0], bmat[u, :, 256:384], ((1,), (1,))) + dot(mask_rows[1], bmat[1 - u, :, 256:384], ((1,), (1,)))
    scale = (pflags[...].astype(f32) / jnp.maximum(count, 1.0)).T
    bias = jnp.zeros((1, 128), f32)
    for i in range(16):
        g32 = cot[i] * scale[:, i:i + 1]
        bias = bias + jnp.sum(g32, axis=0, keepdims=True)
        gmat[:, i * 128:(i + 1) * 128] = g32.astype(bf16)

    for half in range(2):
        db = dot(gmat[...], tmat[half], ((1,), (1,))).astype(bf16)
        for k in range(nblk):
            dstage[k * 2 + half] = db[k * 16:(k + 1) * 16, :]

    def grad_copy(k, t):
        return pltpu.make_async_remote_copy(
            src_ref=dstage.at[t], dst_ref=drecv.at[r], send_sem=dsend.at[t], recv_sem=drecv_sem.at[k],
            device_id={"res": u * nblk + t // nsub, "sub": lax.rem(t, nsub)}, device_id_type=MESH)

    def is_self(t):
        return (u * nblk + t // nsub == r) & (lax.rem(t, nsub) == u)

    def send_grad(k, carry):
        t = lax.rem(k + me, nres)

        @pl.when(jnp.logical_not(is_self(t)))
        def _():
            grad_copy(r, t).start()

        @pl.when(is_self(t))
        def _():
            drecv[r] = dstage[t]

        return carry

    lax.fori_loop(0, nres, send_grad, 0)

    bt = [bmat[half, :, 0:256].astype(f32).T.astype(bf16) for half in range(2)]

    def back(p, carry):
        g = gmat[:, pl.ds(pl.multiple_of(p * 256, 256), 256)]
        for half in range(2):
            part = dot(bt[half], g)
            for d in range(32):
                rows = part[d * 8:(d + 1) * 8, :]
                pair_rows = jnp.concatenate([rows[:, :128], rows[:, 128:]], axis=0)
                dmat[half, pl.ds(pl.multiple_of(p * 16, 16), 16), d * 128:(d + 1) * 128] = pair_rows.astype(bf16)
        return carry

    lax.fori_loop(0, 8, back, 0)

    at_mine = mine_left.T[0:32].astype(bf16)
    at_other = other_left.T[0:32].astype(bf16)
    for q in range(8):
        lanes = slice(q * 512, (q + 1) * 512)
        part = dot(at_mine, dmat[u, :, lanes]) + dot(at_other, dmat[1 - u, :, lanes])
        for k in range(4):
            ostage[q * 4 + k] = part[:, k * 128:(k + 1) * 128].astype(bf16)

    def weight_copy(dst, src):
        return pltpu.make_async_remote_copy(
            src_ref=ostage.at[dst], dst_ref=orecv.at[src], send_sem=osend.at[dst], recv_sem=orecv_sem.at[src],
            device_id=place(dst), device_id_type=MESH)

    def send_weight(k, carry):
        weight_copy(lax.rem(me + k, n), me).start()
        return carry

    lax.fori_loop(1, n, send_weight, 0)
    orecv[me] = ostage[me]

    da_send[...] = dot(dmat[1 - u], wm[...], ((1,), (1,)))

    def da_copy():
        return pltpu.make_async_remote_copy(
            src_ref=da_send, dst_ref=da_recv, send_sem=psend.at[1], recv_sem=precv.at[1],
            device_id={"res": r, "sub": 1 - u}, device_id_type=MESH)

    da_copy().start()
    da = dot(dmat[u], wm[...], ((1,), (1,)))

    for p in range(8):
        lanes = slice(p * 256, (p + 1) * 256)
        z = dot(bmat[0, :, 0:256], tmat[0, :, lanes]) + dot(bmat[1, :, 0:256], tmat[1, :, lanes])
        for k in range(2):
            i = p * 2 + k
            pair[i] = ((z[:, k * 128:(k + 1) * 128] + offset[...]) * scale[:, i:i + 1]).astype(bf16)

    da_copy().wait()

    def wait_grad(k, carry):
        @pl.when((k != r) | (home != u))
        def _():
            grad_copy(k, 0).wait_recv()

        return carry

    lax.fori_loop(0, nres, wait_grad, 0)
    total = drecv[0].astype(f32)
    for k in range(1, nres):
        total = total + drecv[k].astype(f32)
    highest = lax.Precision.HIGHEST
    wide_rows = dot(onehot((128, 16), lambda a, b: a // 8 == b), total, precision=highest) * keep[:, :256]
    db_rows = dot(wide_rows, onehot((256, 128), lambda a, b: b % 64 == 32 + a // 8), precision=highest)
    dfeat = ((da + da_recv[...] + db_rows) * mask).astype(bf16)
    grads = dot(normed16, dfeat, ((0,), (0,)))
    low = lax.broadcasted_iota(jnp.int32, (32, 128), 1) < 64
    small[0:32] = jnp.where(low, grads[0:32], grads[32:64]).astype(bf16)
    small[32:48] = jnp.broadcast_to(bias, (16, 128)).astype(bf16)

    def small_copy(dst, src):
        return pltpu.make_async_remote_copy(
            src_ref=small, dst_ref=small_recv.at[src], send_sem=wsend.at[dst], recv_sem=wrecv.at[src],
            device_id=place(dst), device_id_type=MESH)

    def send_small(k, carry):
        small_copy(lax.rem(me + k, n), me).start()
        return carry

    lax.fori_loop(1, n, send_small, 0)
    small_recv[me] = small[...]

    def wait_weight(k, carry):
        weight_copy(0, lax.rem(me + k, n)).wait_recv()
        return carry

    lax.fori_loop(1, n, wait_weight, 0)
    owned = lax.fori_loop(1, n, lambda k, t: t + orecv[k].astype(f32), orecv[0].astype(f32))
    ogather[me] = owned.astype(bf16)

    def gather_copy(dst, src):
        return pltpu.make_async_remote_copy(
            src_ref=ogather.at[me], dst_ref=ogather.at[src], send_sem=gsend.at[dst], recv_sem=grecv.at[src],
            device_id=place(dst), device_id_type=MESH)

    def send_gather(k, carry):
        gather_copy(lax.rem(me + k, n), me).start()
        return carry

    lax.fori_loop(1, n, send_gather, 0)

    dnormed = dot(dfeat, wab[...], ((1,), (1,)))
    rows_out[...] = inv_std * (
        dnormed - jnp.mean(dnormed, axis=-1, keepdims=True)
        - normed * jnp.mean(dnormed * normed, axis=-1, keepdims=True))
    for s in range(8):
        align[s] = rows_out[pl.ds(s, 16, stride=8), :]

    def wait_small(k, carry):
        small_copy(0, lax.rem(me + k, n)).wait_recv()
        return carry

    lax.fori_loop(1, n, wait_small, 0)
    inv = 1.0 / (16 * nres)
    sums = lax.fori_loop(1, n, lambda k, t: t + small_recv[k].astype(f32), small_recv[0].astype(f32)) * inv
    wa_out[0:32] = sums[0:32, 0:32]
    wa_out[32:64] = sums[0:32, 64:96]
    wb_out[0:32] = sums[0:32, 32:64]
    wb_out[32:64] = sums[0:32, 96:128]
    bias_out[...] = sums[32:33]

    def wait_gather(k, carry):
        gather_copy(0, lax.rem(me + k, n)).wait_recv()
        return carry

    lax.fori_loop(1, n, wait_gather, 0)
    for d in range(32):
        lin_out[pl.ds(d, 32, stride=32), :] = ogather[d].astype(f32) * inv

    def drain(k, carry):
        dst = lax.rem(me + k, n)
        weight_copy(dst, me).wait_send()
        small_copy(dst, me).wait_send()
        gather_copy(dst, me).wait_send()
        return carry

    lax.fori_loop(1, n, drain, 0)

    def drain_near(k, carry):
        @pl.when((k != 0) | (home != u))
        def _():
            block_copy(k).wait_send()

        @pl.when(jnp.logical_not(is_self(k)))
        def _():
            grad_copy(r, k).wait_send()

        return carry

    lax.fori_loop(0, nres, drain_near, 0)


def fused(
    nres, nsub,
    sequence_embedding,
    sequence_present_flags,
    position_couple_flags,
    first_factor_matrix,
    second_factor_matrix,
    final_linear_matrix,
    final_offset_vector,
    couple_change_cotangent,
):
    bf16, f32 = jnp.bfloat16, jnp.float32
    n = nres * nsub
    zeros = jnp.zeros((64, 64), bf16)
    wab = jnp.concatenate([first_factor_matrix, second_factor_matrix, zeros], axis=1)
    vmem = pl.BlockSpec(memory_space=pltpu.VMEM)
    dma = pltpu.SemaphoreType.DMA
    outs = pl.pallas_call(
        functools.partial(kernel, nres, nsub),
        out_shape=(
            jax.ShapeDtypeStruct((16, 128, 128), bf16),
            jax.ShapeDtypeStruct((8, 16, 64), f32),
            jax.ShapeDtypeStruct((64, 32), f32),
            jax.ShapeDtypeStruct((64, 32), f32),
            jax.ShapeDtypeStruct((1024, 128), f32),
            jax.ShapeDtypeStruct((1, 128), f32),
        ),
        in_specs=[vmem] * 6 + [pl.BlockSpec(memory_space=pl.ANY)],
        out_specs=(vmem,) * 6,
        scratch_shapes=[
            pltpu.VMEM((16, 128, 128), f32),
            pltpu.VMEM((128, 128), bf16),
            pltpu.VMEM((128, 128), bf16),
            pltpu.VMEM((16, 384), bf16),
            pltpu.VMEM((2, 128, 384), bf16),
            pltpu.VMEM((128, 4096), bf16),
            pltpu.VMEM((1024, 128), f32),
            pltpu.VMEM((2, 256, 2048), bf16),
            pltpu.VMEM((128, 2048), bf16),
            pltpu.VMEM((2, 128, 4096), bf16),
            pltpu.VMEM((8, 128), f32),
            pltpu.VMEM((nres, 16, 256), bf16),
            pltpu.VMEM((nres, 16, 256), bf16),
            pltpu.VMEM((n, 32, 128), bf16),
            pltpu.VMEM((n, 32, 128), bf16),
            pltpu.VMEM((n, 32, 128), bf16),
            pltpu.VMEM((128, 128), f32),
            pltpu.VMEM((128, 128), f32),
            pltpu.VMEM((48, 128), bf16),
            pltpu.VMEM((n, 48, 128), bf16),
            pltpu.VMEM((128, 64), f32),
            dma,
            dma((nres,)), dma((nres,)),
            dma((nres,)), dma((nres,)),
            dma((n,)), dma((n,)),
            dma((n,)), dma((n,)),
            dma((n,)), dma((n,)),
            dma((2,)), dma((2,)),
        ],
        compiler_params=pltpu.CompilerParams(
            collective_id=0, has_side_effects=True, vmem_limit_bytes=48 * 1024 * 1024
        ),
    )(
        sequence_embedding, sequence_present_flags, position_couple_flags, wab,
        final_linear_matrix, final_offset_vector.reshape(1, 128), couple_change_cotangent,
    )
    return (*outs[:5], outs[5].reshape(128))


def body(
    sequence_embedding,
    sequence_present_flags,
    position_couple_flags,
    first_factor_matrix,
    second_factor_matrix,
    final_linear_matrix,
    final_offset_vector,
    couple_change_cotangent,
):
    highest = lax.Precision.HIGHEST
    precise_scalar = jnp.float32
    hidden = first_factor_matrix.shape[1]
    pair_width = final_linear_matrix.shape[1]
    position_span = sequence_embedding.shape[1]
    col_width = couple_change_cotangent.shape[1]
    col_start = lax.axis_index("sub") * col_width
    present_count_items = sequence_embedding.astype(precise_scalar)
    centred = present_count_items - jnp.mean(present_count_items, axis=-1, keepdims=True)
    variance = jnp.mean(centred * centred, axis=-1, keepdims=True)
    reciprocal_deviation = lax.rsqrt(variance + 1e-05)
    normalized_input = centred * reciprocal_deviation
    layer_scaled_half = normalized_input.astype(jnp.bfloat16)
    row_presence_mask = sequence_present_flags.astype(precise_scalar)[:, None, :]
    first_factor_features = jnp.einsum(
        "sim,mc->sci", layer_scaled_half, first_factor_matrix, preferred_element_type=precise_scalar
    )
    second_factor_features = jnp.einsum(
        "sim,mc->sci",
        layer_scaled_half,
        second_factor_matrix,
        preferred_element_type=precise_scalar,
    )
    feat_a = (first_factor_features * row_presence_mask).astype(jnp.bfloat16)
    feat_b = (second_factor_features * row_presence_mask).astype(jnp.bfloat16)
    mask16 = row_presence_mask.astype(jnp.bfloat16)
    all_a, all_b, all_mask = (
        lax.all_gather(feat_a, "sub", axis=0, tiled=True),
        lax.all_gather(feat_b, "sub", axis=0, tiled=True),
        lax.all_gather(mask16, "sub", axis=0, tiled=True),
    )
    wide_b, wide_mask = (
        lax.all_gather(all_b, "res", axis=2, tiled=True),
        lax.all_gather(all_mask, "res", axis=2, tiled=True),
    )
    col_b = lax.dynamic_slice_in_dim(wide_b, col_start, col_width, 2)
    col_mask = lax.dynamic_slice_in_dim(wide_mask, col_start, col_width, 2)
    pair_count = jnp.einsum(
        "sxi,sxj->ij", all_mask, col_mask, preferred_element_type=precise_scalar
    )
    divisor = jnp.maximum(pair_count, 1.0)[:, :, None]
    out_cube = final_linear_matrix.reshape(hidden, hidden, pair_width)
    tmix = jnp.einsum(
        "sci,cde->side", all_a, out_cube, preferred_element_type=precise_scalar
    ).astype(jnp.bfloat16)
    zsum = jnp.einsum("side,sdj->ije", tmix, col_b, preferred_element_type=precise_scalar)
    pmask = position_couple_flags.astype(precise_scalar)[:, :, None]
    pair_delta_output = (pmask * (zsum + final_offset_vector) / divisor).astype(jnp.bfloat16)
    gscaled32 = couple_change_cotangent * pmask / divisor
    bias_part = jnp.sum(gscaled32, axis=(0, 1))
    gscaled = gscaled32.astype(jnp.bfloat16)
    dtmix = jnp.einsum("ije,sdj->side", gscaled, col_b, preferred_element_type=precise_scalar)
    db_part = jnp.einsum("ije,side->sdj", gscaled, tmix, preferred_element_type=precise_scalar)
    cube_f32 = out_cube.astype(precise_scalar)
    da_part = jnp.einsum("side,cde->sci", dtmix, cube_f32, precision=highest)
    out_part = jnp.einsum("sci,side->cde", all_a.astype(precise_scalar), dtmix, precision=highest)
    placed = jnp.zeros((db_part.shape[0], hidden, wide_b.shape[2]), precise_scalar)
    placed = lax.dynamic_update_slice_in_dim(placed, db_part, col_start, 2)
    res_totals = lax.psum_scatter(placed, "res", scatter_dimension=2, tiled=True)
    da_rows, db_rows = (
        lax.psum_scatter(da_part, "sub", scatter_dimension=0, tiled=True),
        lax.psum_scatter(res_totals, "sub", scatter_dimension=0, tiled=True),
    )
    dfeat_a = da_rows * row_presence_mask
    dfeat_b = db_rows * row_presence_mask
    normed_f = layer_scaled_half.astype(precise_scalar)
    wa_part = jnp.einsum("sim,sci->mc", normed_f, dfeat_a, precision=highest)
    wb_part = jnp.einsum("sim,sci->mc", normed_f, dfeat_b, precision=highest)
    totals = lax.psum((out_part, bias_part, wa_part, wb_part), ("res", "sub"))
    inv_res = 1.0 / (position_span * lax.axis_size("res"))
    output_weight_gradient = totals[0].reshape(hidden * hidden, pair_width) * inv_res
    output_bias_gradient = totals[1] * inv_res
    left_weight_gradient = totals[2] * inv_res
    right_weight_gradient = totals[3] * inv_res
    normalized_gradient = jnp.einsum(
        "sci,mc->sim", dfeat_a, first_factor_matrix.astype(precise_scalar), precision=highest
    )
    normalized_gradient = normalized_gradient + jnp.einsum(
        "sci,mc->sim", dfeat_b, second_factor_matrix.astype(precise_scalar), precision=highest
    )
    alignment_gradient = reciprocal_deviation * (
        normalized_gradient
        - jnp.mean(normalized_gradient, axis=-1, keepdims=True)
        - normalized_input
        * jnp.mean(normalized_gradient * normalized_input, axis=-1, keepdims=True)
    )
    return (
        pair_delta_output,
        alignment_gradient,
        left_weight_gradient,
        right_weight_gradient,
        output_weight_gradient,
        output_bias_gradient,
    )


def solution(mesh):
    in_specs = (
        P("sub", ("groups", "res"), None),
        P("sub", ("groups", "res")),
        P(("groups", "res"), "sub"),
        P(),
        P(),
        P(),
        P(),
        P(("groups", "res"), "sub", None),
    )
    out_specs = (
        P(("groups", "res"), "sub", None),
        P("sub", ("groups", "res"), None),
        P("groups", None),
        P("groups", None),
        P("groups", None),
        P("groups"),
    )
    nres, nsub = mesh.shape["res"], mesh.shape["sub"]
    chosen = functools.partial(fused, nres, nsub) if (nres, nsub) == (16, 2) else body
    return jax.shard_map(chosen, mesh=mesh, in_specs=in_specs, out_specs=out_specs, check_vma=False)
```

```python
import functools

import jax
import jax.numpy as jnp
from jax import lax
from jax.sharding import PartitionSpec as P
from jax.experimental import pallas as pl
from jax.experimental.pallas import tpu as pltpu


MESH = pl.DeviceIdType.MESH


def onehot(shape, test):
    rows = lax.broadcasted_iota(jnp.int32, shape, 0)
    lanes = lax.broadcasted_iota(jnp.int32, shape, 1)
    return jnp.where(test(rows, lanes), 1.0, 0.0)


def dot(a, b, dims=((1,), (0,)), precision=None):
    return lax.dot_general(a, b, (dims, ((), ())), preferred_element_type=jnp.float32, precision=precision)


def kernel(
    nres, nsub,
    emb_hbm, flags_hbm, pflags_hbm, wa_hbm, wb_hbm, lin_hbm, offset_hbm, cot_hbm,
    pair, align, wa_out, wb_out, lin_out, bias_out,
    emb, flags, pflags, wa_t, wb_t, lin, offset, cot, feat, other, blk, bmat, wm, lin32, tmat, gmat, dmat, dstage, drecv,
    ostage, orecv, ogather, da_send, da_recv, small, small_recv, plane, plane_recv, rows_out,
    in_sem, bsend, brecv, dsend, drecv_sem, osend, orecv_sem, gsend, grecv, wsend, wrecv, psend, precv, vsend, vrecv,
):
    bf16, f32 = jnp.bfloat16, jnp.float32
    n = nres * nsub
    nblk = nres // nsub
    r, u = lax.axis_index("res"), lax.axis_index("sub")
    me = r * nsub + u

    def place(k):
        return {"res": k // nsub, "sub": lax.rem(k, nsub)}

    ins = [
        pltpu.make_async_copy(a, b, in_sem.at[k])
        for k, (a, b) in enumerate([
            (emb_hbm, emb), (flags_hbm, flags), (wa_hbm, wa_t), (wb_hbm, wb_t),
            (lin_hbm, lin), (pflags_hbm, pflags), (offset_hbm, offset), (cot_hbm, cot)])
    ]
    for copy in ins:
        copy.start()
    near = 8
    far = n // near
    spot, layer = lax.rem(me, near), me // near
    barrier = pltpu.get_barrier_semaphore()

    def greet(k, carry):
        pl.semaphore_signal(barrier, inc=1, device_id=place(lax.rem(me + k, n)), device_id_type=MESH)
        return carry

    lax.fori_loop(1, n, greet, 0)

    for copy in ins[:4]:
        copy.wait()
    wab_t = jnp.concatenate([wa_t[...], wb_t[...], jnp.zeros((64, 64), bf16)], axis=0)

    x = dot(onehot((128, 128), lambda a, b: b == (a % 8) * 16 + a // 8).astype(bf16), emb[...].reshape(128, 64))
    centred = x - jnp.mean(x, axis=-1, keepdims=True)
    inv_std = lax.rsqrt(jnp.mean(centred * centred, axis=-1, keepdims=True) + 1e-05)
    normed = centred * inv_std
    normed16 = normed.astype(bf16)
    picked = dot(onehot((128, 8), lambda a, b: a % 8 == b).astype(bf16), flags[...].astype(f32).astype(bf16))
    mask = jnp.sum(picked * onehot((128, 16), lambda a, b: a // 8 == b), axis=1, keepdims=True)
    projected = dot(normed16, wab_t, ((1,), (1,))) * mask
    projected = projected + mask * onehot((128, 128), lambda a, b: b - 64 == a % 8)
    feat[...] = projected.astype(bf16)
    keep = onehot((128, 384), lambda a, b: a % 8 == b % 8)
    spread = onehot((128, 384), lambda a, b: ((b < 256) & (a == 32 + b // 8)) | ((a >= 64) & (b - 256 == a)))
    gather_rows = onehot((16, 128), lambda a, b: a == b // 8).astype(bf16)
    mine = dot(gather_rows, (dot(feat[...], spread.astype(bf16)) * keep).astype(bf16)).astype(bf16)
    blk[...] = mine
    home = r // nblk
    slot = u * nblk + lax.rem(r, nblk)
    rows_here = pl.ds(pl.multiple_of(lax.rem(r, nblk) * 16, 16), 16)

    pl.semaphore_wait(barrier, n - 1)

    def partner_copy():
        return pltpu.make_async_remote_copy(
            src_ref=feat, dst_ref=other, send_sem=psend.at[0], recv_sem=precv.at[0],
            device_id={"res": r, "sub": 1 - u}, device_id_type=MESH)

    partner_copy().start()

    def block_copy(k):
        q = lax.rem(r + k, nres)
        return pltpu.make_async_remote_copy(
            src_ref=blk, dst_ref=bmat.at[u, rows_here, :], send_sem=bsend.at[k], recv_sem=brecv.at[slot],
            device_id={"res": q, "sub": home}, device_id_type=MESH)

    def send_block(k, carry):
        block_copy(k).start()
        return carry

    lax.fori_loop(1, nres, send_block, 0)

    @pl.when(home != u)
    def _():
        block_copy(0).start()

    @pl.when(home == u)
    def _():
        bmat[u, rows_here, :] = mine

    ins[4].wait()
    lin32[...] = lin[...].astype(f32)
    wm[...] = jnp.zeros_like(wm)
    for d in range(32):
        piece = lin32[pl.ds(d, 32, stride=32), :].astype(bf16)
        wm[0:32, d * 128:(d + 1) * 128] = piece
        wm[64:96, d * 128:(d + 1) * 128] = piece

    lane128 = lax.broadcasted_iota(jnp.int32, (128, 128), 1)

    def left_only(ref):
        return jnp.where(lane128 < 32, ref[...].astype(f32), 0.0)

    def mix(half, left):
        for p in range(16):
            part = dot(left, wm[:, p * 256:(p + 1) * 256])
            for i in range(16):
                rows = part[i * 8:(i + 1) * 8, :]
                pair_rows = jnp.concatenate([rows[:, :128], rows[:, 128:]], axis=0)
                tmat[half, p * 16:(p + 1) * 16, i * 128:(i + 1) * 128] = pair_rows.astype(bf16)

    mine_left = left_only(feat)
    mix(u, mine_left.astype(bf16))
    partner_copy().wait()
    other_left = left_only(other)
    mix(1 - u, other_left.astype(bf16))

    mask_rows = [dot(gather_rows, ref[...]).astype(bf16) for ref in (feat, other)]

    for copy in ins[5:]:
        copy.wait()

    def wait_block(k, carry):
        @pl.when(k != slot)
        def _():
            copy = pltpu.make_async_remote_copy(
                src_ref=blk, dst_ref=bmat.at[k // nblk, pl.ds(pl.multiple_of(lax.rem(k, nblk) * 16, 16), 16), :],
                send_sem=bsend.at[0], recv_sem=brecv.at[k], device_id={"res": r, "sub": 1 - u}, device_id_type=MESH)
            copy.wait_recv()

        @pl.when((k == slot) & (home != u))
        def _():
            copy = pltpu.make_async_remote_copy(
                src_ref=blk, dst_ref=bmat.at[k // nblk, pl.ds(pl.multiple_of(lax.rem(k, nblk) * 16, 16), 16), :],
                send_sem=bsend.at[0], recv_sem=brecv.at[k], device_id={"res": r, "sub": 1 - u}, device_id_type=MESH)
            copy.wait_recv()

        return carry

    lax.fori_loop(0, nres, wait_block, 0)

    count = dot(mask_rows[0], bmat[u, :, 256:384], ((1,), (1,))) + dot(mask_rows[1], bmat[1 - u, :, 256:384], ((1,), (1,)))
    scale = (pflags[...].astype(f32) / jnp.maximum(count, 1.0)).T
    bias = jnp.zeros((1, 128), f32)
    for i in range(16):
        g32 = cot[i] * scale[:, i:i + 1]
        bias = bias + jnp.sum(g32, axis=0, keepdims=True)
        gmat[:, i * 128:(i + 1) * 128] = g32.astype(bf16)

    for half in range(2):
        db = dot(gmat[...], tmat[half], ((1,), (1,))).astype(bf16)
        for k in range(nblk):
            dstage[k * 2 + half] = db[k * 16:(k + 1) * 16, :]

    def grad_copy(k, t):
        return pltpu.make_async_remote_copy(
            src_ref=dstage.at[t], dst_ref=drecv.at[r], send_sem=dsend.at[t], recv_sem=drecv_sem.at[k],
            device_id={"res": u * nblk + t // nsub, "sub": lax.rem(t, nsub)}, device_id_type=MESH)

    def is_self(t):
        return (u * nblk + t // nsub == r) & (lax.rem(t, nsub) == u)

    def send_grad(k, carry):
        t = lax.rem(k + me, nres)

        @pl.when(jnp.logical_not(is_self(t)))
        def _():
            grad_copy(r, t).start()

        @pl.when(is_self(t))
        def _():
            drecv[r] = dstage[t]

        return carry

    lax.fori_loop(0, nres, send_grad, 0)

    bt = [bmat[half, :, 0:256].astype(f32).T.astype(bf16) for half in range(2)]

    for p in range(8):
        g = gmat[:, p * 256:(p + 1) * 256]
        for half in range(2):
            part = dot(bt[half], g)
            for d in range(32):
                rows = part[d * 8:(d + 1) * 8, :]
                pair_rows = jnp.concatenate([rows[:, :128], rows[:, 128:]], axis=0)
                dmat[half, p * 16:(p + 1) * 16, d * 128:(d + 1) * 128] = pair_rows.astype(bf16)

    at_mine = mine_left.T[0:32].astype(bf16)
    at_other = other_left.T[0:32].astype(bf16)
    for q in range(8):
        lanes = slice(q * 512, (q + 1) * 512)
        part = dot(at_mine, dmat[u, :, lanes]) + dot(at_other, dmat[1 - u, :, lanes])
        for k in range(4):
            ostage[q * 4 + k] = part[:, k * 128:(k + 1) * 128].astype(bf16)

    def weight_copy(dst, src):
        return pltpu.make_async_remote_copy(
            src_ref=ostage.at[dst], dst_ref=orecv.at[src], send_sem=osend.at[dst], recv_sem=orecv_sem.at[src],
            device_id=place(dst), device_id_type=MESH)

    def send_weight(k, carry):
        weight_copy(lax.rem(me + k, n), me).start()
        return carry

    lax.fori_loop(1, n, send_weight, 0)
    orecv[me] = ostage[me]

    da_send[...] = dot(dmat[1 - u], wm[...], ((1,), (1,)))

    def da_copy():
        return pltpu.make_async_remote_copy(
            src_ref=da_send, dst_ref=da_recv, send_sem=psend.at[1], recv_sem=precv.at[1],
            device_id={"res": r, "sub": 1 - u}, device_id_type=MESH)

    da_copy().start()
    da = dot(dmat[u], wm[...], ((1,), (1,)))

    for p in range(8):
        lanes = slice(p * 256, (p + 1) * 256)
        z = dot(bmat[0, :, 0:256], tmat[0, :, lanes]) + dot(bmat[1, :, 0:256], tmat[1, :, lanes])
        for k in range(2):
            i = p * 2 + k
            pair[i] = ((z[:, k * 128:(k + 1) * 128] + offset[...]) * scale[:, i:i + 1]).astype(bf16)

    da_copy().wait()

    def wait_grad(k, carry):
        @pl.when((k != r) | (home != u))
        def _():
            grad_copy(k, 0).wait_recv()

        return carry

    lax.fori_loop(0, nres, wait_grad, 0)
    total = drecv[0].astype(f32)
    for k in range(1, nres):
        total = total + drecv[k].astype(f32)
    highest = lax.Precision.HIGHEST
    wide_rows = dot(onehot((128, 16), lambda a, b: a // 8 == b), total, precision=highest) * keep[:, :256]
    db_rows = dot(wide_rows, onehot((256, 128), lambda a, b: b % 64 == 32 + a // 8), precision=highest)
    dfeat = ((da + da_recv[...] + db_rows) * mask).astype(bf16)
    twice = dot(normed16, onehot((64, 128), lambda a, b: b % 64 == a).astype(bf16)).astype(bf16)
    grads = dot(dfeat, twice, ((0,), (0,)))
    low = lax.broadcasted_iota(jnp.int32, (32, 128), 1) < 64
    small[0:32] = jnp.where(low, grads[0:32], grads[32:64]).astype(bf16)
    small[32:48] = jnp.broadcast_to(bias, (16, 128)).astype(bf16)

    def small_copy(dst, src):
        return pltpu.make_async_remote_copy(
            src_ref=small, dst_ref=small_recv.at[src], send_sem=wsend.at[dst], recv_sem=wrecv.at[src],
            device_id=place(layer * near + dst), device_id_type=MESH)

    def plane_copy(dst, src):
        return pltpu.make_async_remote_copy(
            src_ref=plane, dst_ref=plane_recv.at[src], send_sem=vsend.at[dst], recv_sem=vrecv.at[src],
            device_id=place(dst * near + spot), device_id_type=MESH)

    for k in range(1, near):
        small_copy(lax.rem(spot + k, near), spot).start()
    small_recv[spot] = small[...]

    def wait_weight(k, carry):
        weight_copy(0, lax.rem(me + k, n)).wait_recv()
        return carry

    lax.fori_loop(1, n, wait_weight, 0)
    owned = lax.fori_loop(1, n, lambda k, t: t + orecv[k].astype(f32), orecv[0].astype(f32))
    ogather[me] = owned.astype(bf16)

    def gather_copy(dst, src):
        return pltpu.make_async_remote_copy(
            src_ref=ogather.at[me], dst_ref=ogather.at[src], send_sem=gsend.at[dst], recv_sem=grecv.at[src],
            device_id=place(dst), device_id_type=MESH)

    def send_gather(k, carry):
        gather_copy(lax.rem(me + k, n), me).start()
        return carry

    lax.fori_loop(1, n, send_gather, 0)

    for k in range(1, near):
        small_copy(0, lax.rem(spot + k, near)).wait_recv()
    near_sum = small_recv[0].astype(f32)
    for k in range(1, near):
        near_sum = near_sum + small_recv[k].astype(f32)
    plane[...] = near_sum.astype(bf16)
    for k in range(1, far):
        plane_copy(lax.rem(layer + k, far), layer).start()
    plane_recv[layer] = plane[...]

    dnormed = dot(dfeat, wab_t)
    rows_out[...] = inv_std * (
        dnormed - jnp.mean(dnormed, axis=-1, keepdims=True)
        - normed * jnp.mean(dnormed * normed, axis=-1, keepdims=True))
    for s in range(8):
        align[s] = rows_out[pl.ds(s, 16, stride=8), :]

    for k in range(1, far):
        plane_copy(0, lax.rem(layer + k, far)).wait_recv()
    inv = 1.0 / (16 * nres)
    sums = plane_recv[0].astype(f32)
    for k in range(1, far):
        sums = sums + plane_recv[k].astype(f32)
    sums = sums * inv
    wa_out[...] = sums[0:32, 0:64]
    wb_out[...] = sums[0:32, 64:128]
    bias_out[...] = sums[32:33]

    def wait_gather(k, carry):
        gather_copy(0, lax.rem(me + k, n)).wait_recv()
        return carry

    lax.fori_loop(1, n, wait_gather, 0)
    for d in range(32):
        lin_out[pl.ds(d, 32, stride=32), :] = ogather[d].astype(f32) * inv

    def drain(k, carry):
        dst = lax.rem(me + k, n)
        weight_copy(dst, me).wait_send()
        gather_copy(dst, me).wait_send()
        return carry

    lax.fori_loop(1, n, drain, 0)

    for k in range(1, near):
        small_copy(lax.rem(spot + k, near), spot).wait_send()
    for k in range(1, far):
        plane_copy(lax.rem(layer + k, far), layer).wait_send()

    def drain_near(k, carry):
        @pl.when((k != 0) | (home != u))
        def _():
            block_copy(k).wait_send()

        @pl.when(jnp.logical_not(is_self(k)))
        def _():
            grad_copy(r, k).wait_send()

        return carry

    lax.fori_loop(0, nres, drain_near, 0)


def hand_over(*refs):
    sems = refs[-1]
    half = (len(refs) - 1) // 2
    copies = [pltpu.make_async_copy(refs[k], refs[half + k], sems.at[k]) for k in range(half)]
    for copy in copies:
        copy.start()
    for copy in copies:
        copy.wait()


def fused(
    nres, nsub,
    sequence_embedding,
    sequence_present_flags,
    position_couple_flags,
    first_factor_matrix,
    second_factor_matrix,
    final_linear_matrix,
    final_offset_vector,
    couple_change_cotangent,
):
    bf16, f32 = jnp.bfloat16, jnp.float32
    n = nres * nsub
    hbm = pl.BlockSpec(memory_space=pltpu.HBM)
    vmem = pl.BlockSpec(memory_space=pltpu.VMEM)
    dma = pltpu.SemaphoreType.DMA
    shapes = (
        jax.ShapeDtypeStruct((16, 128, 128), bf16),
        jax.ShapeDtypeStruct((8, 16, 64), f32),
        jax.ShapeDtypeStruct((32, 64), f32),
        jax.ShapeDtypeStruct((32, 64), f32),
        jax.ShapeDtypeStruct((1024, 128), f32),
        jax.ShapeDtypeStruct((1, 128), f32),
    )
    operands = (
        sequence_embedding, sequence_present_flags, position_couple_flags,
        first_factor_matrix.T, second_factor_matrix.T,
        final_linear_matrix, final_offset_vector.reshape(1, 128), couple_change_cotangent,
    )
    outs = pl.pallas_call(
        functools.partial(kernel, nres, nsub),
        out_shape=shapes,
        in_specs=[hbm] * 8,
        out_specs=(vmem,) * 6,
        scratch_shapes=[pltpu.VMEM(a.shape, a.dtype) for a in operands] + [
            pltpu.VMEM((128, 128), bf16),
            pltpu.VMEM((128, 128), bf16),
            pltpu.VMEM((16, 384), bf16),
            pltpu.VMEM((2, 128, 384), bf16),
            pltpu.VMEM((128, 4096), bf16),
            pltpu.VMEM((1024, 128), f32),
            pltpu.VMEM((2, 256, 2048), bf16),
            pltpu.VMEM((128, 2048), bf16),
            pltpu.VMEM((2, 128, 4096), bf16),
            pltpu.VMEM((nres, 16, 256), bf16),
            pltpu.VMEM((nres, 16, 256), bf16),
            pltpu.VMEM((n, 32, 128), bf16),
            pltpu.VMEM((n, 32, 128), bf16),
            pltpu.VMEM((n, 32, 128), bf16),
            pltpu.VMEM((128, 128), f32),
            pltpu.VMEM((128, 128), f32),
            pltpu.VMEM((48, 128), bf16),
            pltpu.VMEM((8, 48, 128), bf16),
            pltpu.VMEM((48, 128), bf16),
            pltpu.VMEM((n // 8, 48, 128), bf16),
            pltpu.VMEM((128, 64), f32),
            dma((8,)),
            dma((nres,)), dma((nres,)),
            dma((nres,)), dma((nres,)),
            dma((n,)), dma((n,)),
            dma((n,)), dma((n,)),
            dma((8,)), dma((8,)),
            dma((2,)), dma((2,)),
            dma((n // 8,)), dma((n // 8,)),
        ],
        compiler_params=pltpu.CompilerParams(
            collective_id=0, has_side_effects=True, vmem_limit_bytes=40 * 1024 * 1024
        ),
    )(*operands)
    outs = pl.pallas_call(
        hand_over,
        out_shape=shapes,
        in_specs=[vmem] * 6,
        out_specs=(hbm,) * 6,
        scratch_shapes=[dma((6,))],
        compiler_params=pltpu.CompilerParams(vmem_limit_bytes=32 * 1024 * 1024),
    )(*outs)
    return (outs[0], outs[1], outs[2].T, outs[3].T, outs[4], outs[5].reshape(128))


def body(
    sequence_embedding,
    sequence_present_flags,
    position_couple_flags,
    first_factor_matrix,
    second_factor_matrix,
    final_linear_matrix,
    final_offset_vector,
    couple_change_cotangent,
):
    highest = lax.Precision.HIGHEST
    precise_scalar = jnp.float32
    hidden = first_factor_matrix.shape[1]
    pair_width = final_linear_matrix.shape[1]
    position_span = sequence_embedding.shape[1]
    col_width = couple_change_cotangent.shape[1]
    col_start = lax.axis_index("sub") * col_width
    present_count_items = sequence_embedding.astype(precise_scalar)
    centred = present_count_items - jnp.mean(present_count_items, axis=-1, keepdims=True)
    variance = jnp.mean(centred * centred, axis=-1, keepdims=True)
    reciprocal_deviation = lax.rsqrt(variance + 1e-05)
    normalized_input = centred * reciprocal_deviation
    layer_scaled_half = normalized_input.astype(jnp.bfloat16)
    row_presence_mask = sequence_present_flags.astype(precise_scalar)[:, None, :]
    first_factor_features = jnp.einsum(
        "sim,mc->sci", layer_scaled_half, first_factor_matrix, preferred_element_type=precise_scalar
    )
    second_factor_features = jnp.einsum(
        "sim,mc->sci",
        layer_scaled_half,
        second_factor_matrix,
        preferred_element_type=precise_scalar,
    )
    feat_a = (first_factor_features * row_presence_mask).astype(jnp.bfloat16)
    feat_b = (second_factor_features * row_presence_mask).astype(jnp.bfloat16)
    mask16 = row_presence_mask.astype(jnp.bfloat16)
    all_a, all_b, all_mask = (
        lax.all_gather(feat_a, "sub", axis=0, tiled=True),
        lax.all_gather(feat_b, "sub", axis=0, tiled=True),
        lax.all_gather(mask16, "sub", axis=0, tiled=True),
    )
    wide_b, wide_mask = (
        lax.all_gather(all_b, "res", axis=2, tiled=True),
        lax.all_gather(all_mask, "res", axis=2, tiled=True),
    )
    col_b = lax.dynamic_slice_in_dim(wide_b, col_start, col_width, 2)
    col_mask = lax.dynamic_slice_in_dim(wide_mask, col_start, col_width, 2)
    pair_count = jnp.einsum(
        "sxi,sxj->ij", all_mask, col_mask, preferred_element_type=precise_scalar
    )
    divisor = jnp.maximum(pair_count, 1.0)[:, :, None]
    out_cube = final_linear_matrix.reshape(hidden, hidden, pair_width)
    tmix = jnp.einsum(
        "sci,cde->side", all_a, out_cube, preferred_element_type=precise_scalar
    ).astype(jnp.bfloat16)
    zsum = jnp.einsum("side,sdj->ije", tmix, col_b, preferred_element_type=precise_scalar)
    pmask = position_couple_flags.astype(precise_scalar)[:, :, None]
    pair_delta_output = (pmask * (zsum + final_offset_vector) / divisor).astype(jnp.bfloat16)
    gscaled32 = couple_change_cotangent * pmask / divisor
    bias_part = jnp.sum(gscaled32, axis=(0, 1))
    gscaled = gscaled32.astype(jnp.bfloat16)
    dtmix = jnp.einsum("ije,sdj->side", gscaled, col_b, preferred_element_type=precise_scalar)
    db_part = jnp.einsum("ije,side->sdj", gscaled, tmix, preferred_element_type=precise_scalar)
    cube_f32 = out_cube.astype(precise_scalar)
    da_part = jnp.einsum("side,cde->sci", dtmix, cube_f32, precision=highest)
    out_part = jnp.einsum("sci,side->cde", all_a.astype(precise_scalar), dtmix, precision=highest)
    placed = jnp.zeros((db_part.shape[0], hidden, wide_b.shape[2]), precise_scalar)
    placed = lax.dynamic_update_slice_in_dim(placed, db_part, col_start, 2)
    res_totals = lax.psum_scatter(placed, "res", scatter_dimension=2, tiled=True)
    da_rows, db_rows = (
        lax.psum_scatter(da_part, "sub", scatter_dimension=0, tiled=True),
        lax.psum_scatter(res_totals, "sub", scatter_dimension=0, tiled=True),
    )
    dfeat_a = da_rows * row_presence_mask
    dfeat_b = db_rows * row_presence_mask
    normed_f = layer_scaled_half.astype(precise_scalar)
    wa_part = jnp.einsum("sim,sci->mc", normed_f, dfeat_a, precision=highest)
    wb_part = jnp.einsum("sim,sci->mc", normed_f, dfeat_b, precision=highest)
    totals = lax.psum((out_part, bias_part, wa_part, wb_part), ("res", "sub"))
    inv_res = 1.0 / (position_span * lax.axis_size("res"))
    output_weight_gradient = totals[0].reshape(hidden * hidden, pair_width) * inv_res
    output_bias_gradient = totals[1] * inv_res
    left_weight_gradient = totals[2] * inv_res
    right_weight_gradient = totals[3] * inv_res
    normalized_gradient = jnp.einsum(
        "sci,mc->sim", dfeat_a, first_factor_matrix.astype(precise_scalar), precision=highest
    )
    normalized_gradient = normalized_gradient + jnp.einsum(
        "sci,mc->sim", dfeat_b, second_factor_matrix.astype(precise_scalar), precision=highest
    )
    alignment_gradient = reciprocal_deviation * (
        normalized_gradient
        - jnp.mean(normalized_gradient, axis=-1, keepdims=True)
        - normalized_input
        * jnp.mean(normalized_gradient * normalized_input, axis=-1, keepdims=True)
    )
    return (
        pair_delta_output,
        alignment_gradient,
        left_weight_gradient,
        right_weight_gradient,
        output_weight_gradient,
        output_bias_gradient,
    )


def solution(mesh):
    in_specs = (
        P("sub", ("groups", "res"), None),
        P("sub", ("groups", "res")),
        P(("groups", "res"), "sub"),
        P(),
        P(),
        P(),
        P(),
        P(("groups", "res"), "sub", None),
    )
    out_specs = (
        P(("groups", "res"), "sub", None),
        P("sub", ("groups", "res"), None),
        P("groups", None),
        P("groups", None),
        P("groups", None),
        P("groups"),
    )
    nres, nsub = mesh.shape["res"], mesh.shape["sub"]
    chosen = functools.partial(fused, nres, nsub) if (nres, nsub) == (16, 2) else body
    return jax.shard_map(chosen, mesh=mesh, in_specs=in_specs, out_specs=out_specs, check_vma=False)
```

```python
import functools

import jax
import jax.numpy as jnp
from jax import lax
from jax.sharding import PartitionSpec as P
from jax.experimental import pallas as pl
from jax.experimental.pallas import tpu as pltpu


MESH = pl.DeviceIdType.MESH


def onehot(shape, test):
    rows = lax.broadcasted_iota(jnp.int32, shape, 0)
    lanes = lax.broadcasted_iota(jnp.int32, shape, 1)
    return jnp.where(test(rows, lanes), 1.0, 0.0)


def dot(a, b, dims=((1,), (0,)), precision=None):
    return lax.dot_general(a, b, (dims, ((), ())), preferred_element_type=jnp.float32, precision=precision)


def kernel(
    nres, nsub,
    emb_hbm, flags_hbm, pflags_hbm, wa_hbm, wb_hbm, lin_hbm, offset_hbm, cot_hbm,
    pair_hbm, align_hbm, wa_hbm_out, wb_hbm_out, lin_hbm_out, bias_hbm_out,
    emb, flags, pflags, wa_t, wb_t, lin, offset, cot,
    pair, align, wa_out, wb_out, lin_out, bias_out, feat, other, blk, bmat, wm, lin32, tmat, gmat, dmat, dstage, drecv,
    ostage, orecv, ogather, fstage, frecv, owned, da_send, da_recv, small, small_recv, plane, plane_recv, rows_out,
    in_sem, out_sem, bsend, brecv, dsend, drecv_sem, osend, orecv_sem, gsend, grecv, wsend, wrecv, psend, precv, vsend, vrecv, fsend, frecv_sem, hsend, hrecv,
):
    bf16, f32 = jnp.bfloat16, jnp.float32
    n = nres * nsub
    nblk = nres // nsub
    r, u = lax.axis_index("res"), lax.axis_index("sub")
    me = r * nsub + u

    def place(k):
        return {"res": k // nsub, "sub": lax.rem(k, nsub)}

    ins = [
        pltpu.make_async_copy(a, b, in_sem.at[k])
        for k, (a, b) in enumerate([
            (emb_hbm, emb), (flags_hbm, flags), (wa_hbm, wa_t), (wb_hbm, wb_t),
            (lin_hbm, lin), (pflags_hbm, pflags), (offset_hbm, offset), (cot_hbm, cot)])
    ]
    outs = [
        pltpu.make_async_copy(a, b, out_sem.at[k])
        for k, (a, b) in enumerate([
            (pair, pair_hbm), (align, align_hbm), (wa_out, wa_hbm_out),
            (wb_out, wb_hbm_out), (lin_out, lin_hbm_out), (bias_out, bias_hbm_out)])
    ]
    for copy in ins:
        copy.start()
    near = 8
    far = n // near
    spot, layer = lax.rem(me, near), me // near
    barrier = pltpu.get_barrier_semaphore()

    def greet(k, carry):
        pl.semaphore_signal(barrier, inc=1, device_id=place(lax.rem(me + k, n)), device_id_type=MESH)
        return carry

    lax.fori_loop(1, n, greet, 0)

    for copy in ins[:4]:
        copy.wait()
    wab_t = jnp.concatenate([wa_t[...], wb_t[...], jnp.zeros((64, 64), bf16)], axis=0)

    x = dot(onehot((128, 128), lambda a, b: b == (a % 8) * 16 + a // 8).astype(bf16), emb[...].reshape(128, 64))
    centred = x - jnp.mean(x, axis=-1, keepdims=True)
    inv_std = lax.rsqrt(jnp.mean(centred * centred, axis=-1, keepdims=True) + 1e-05)
    normed = centred * inv_std
    normed16 = normed.astype(bf16)
    picked = dot(onehot((128, 8), lambda a, b: a % 8 == b).astype(bf16), flags[...].astype(f32).astype(bf16))
    mask = jnp.sum(picked * onehot((128, 16), lambda a, b: a // 8 == b), axis=1, keepdims=True)
    projected = dot(normed16, wab_t, ((1,), (1,))) * mask
    projected = projected + mask * onehot((128, 128), lambda a, b: b - 64 == a % 8)
    feat[...] = projected.astype(bf16)
    keep = onehot((128, 384), lambda a, b: a % 8 == b % 8)
    spread = onehot((128, 384), lambda a, b: ((b < 256) & (a == 32 + b // 8)) | ((a >= 64) & (b - 256 == a)))
    gather_rows = onehot((16, 128), lambda a, b: a == b // 8).astype(bf16)
    mine = dot(gather_rows, (dot(feat[...], spread.astype(bf16)) * keep).astype(bf16)).astype(bf16)
    blk[...] = mine
    home = r // nblk
    slot = u * nblk + lax.rem(r, nblk)
    rows_here = pl.ds(pl.multiple_of(lax.rem(r, nblk) * 16, 16), 16)

    pl.semaphore_wait(barrier, n - 1)

    def partner_copy():
        return pltpu.make_async_remote_copy(
            src_ref=feat, dst_ref=other, send_sem=psend.at[0], recv_sem=precv.at[0],
            device_id={"res": r, "sub": 1 - u}, device_id_type=MESH)

    partner_copy().start()

    def block_copy(k):
        q = lax.rem(r + k, nres)
        return pltpu.make_async_remote_copy(
            src_ref=blk, dst_ref=bmat.at[u, rows_here, :], send_sem=bsend.at[k], recv_sem=brecv.at[slot],
            device_id={"res": q, "sub": home}, device_id_type=MESH)

    def send_block(k, carry):
        block_copy(k).start()
        return carry

    lax.fori_loop(1, nres, send_block, 0)

    @pl.when(home != u)
    def _():
        block_copy(0).start()

    @pl.when(home == u)
    def _():
        bmat[u, rows_here, :] = mine

    ins[4].wait()
    lin32[...] = lin[...].astype(f32)
    wm[...] = jnp.zeros_like(wm)
    for d in range(32):
        piece = lin32[pl.ds(d, 32, stride=32), :].astype(bf16)
        wm[0:32, d * 128:(d + 1) * 128] = piece
        wm[64:96, d * 128:(d + 1) * 128] = piece

    lane128 = lax.broadcasted_iota(jnp.int32, (128, 128), 1)

    def left_only(ref):
        return jnp.where(lane128 < 32, ref[...].astype(f32), 0.0)

    def mix(half, left):
        for p in range(16):
            part = dot(left, wm[:, p * 256:(p + 1) * 256])
            for i in range(16):
                rows = part[i * 8:(i + 1) * 8, :]
                pair_rows = jnp.concatenate([rows[:, :128], rows[:, 128:]], axis=0)
                tmat[half, p * 16:(p + 1) * 16, i * 128:(i + 1) * 128] = pair_rows.astype(bf16)

    mine_left = left_only(feat)
    mix(u, mine_left.astype(bf16))
    partner_copy().wait()
    other_left = left_only(other)
    mix(1 - u, other_left.astype(bf16))

    mask_rows = [dot(gather_rows, ref[...]).astype(bf16) for ref in (feat, other)]

    for copy in ins[5:]:
        copy.wait()

    def wait_block(k, carry):
        @pl.when(k != slot)
        def _():
            copy = pltpu.make_async_remote_copy(
                src_ref=blk, dst_ref=bmat.at[k // nblk, pl.ds(pl.multiple_of(lax.rem(k, nblk) * 16, 16), 16), :],
                send_sem=bsend.at[0], recv_sem=brecv.at[k], device_id={"res": r, "sub": 1 - u}, device_id_type=MESH)
            copy.wait_recv()

        @pl.when((k == slot) & (home != u))
        def _():
            copy = pltpu.make_async_remote_copy(
                src_ref=blk, dst_ref=bmat.at[k // nblk, pl.ds(pl.multiple_of(lax.rem(k, nblk) * 16, 16), 16), :],
                send_sem=bsend.at[0], recv_sem=brecv.at[k], device_id={"res": r, "sub": 1 - u}, device_id_type=MESH)
            copy.wait_recv()

        return carry

    lax.fori_loop(0, nres, wait_block, 0)

    count = dot(mask_rows[0], bmat[u, :, 256:384], ((1,), (1,))) + dot(mask_rows[1], bmat[1 - u, :, 256:384], ((1,), (1,)))
    scale = (pflags[...].astype(f32) / jnp.maximum(count, 1.0)).T
    bias = jnp.zeros((1, 128), f32)
    for i in range(16):
        g32 = cot[i] * scale[:, i:i + 1]
        bias = bias + jnp.sum(g32, axis=0, keepdims=True)
        gmat[:, i * 128:(i + 1) * 128] = g32.astype(bf16)

    for half in range(2):
        db = dot(gmat[...], tmat[half], ((1,), (1,))).astype(bf16)
        for k in range(nblk):
            dstage[k * 2 + half] = db[k * 16:(k + 1) * 16, :]

    def grad_copy(k, t):
        return pltpu.make_async_remote_copy(
            src_ref=dstage.at[t], dst_ref=drecv.at[r], send_sem=dsend.at[t], recv_sem=drecv_sem.at[k],
            device_id={"res": u * nblk + t // nsub, "sub": lax.rem(t, nsub)}, device_id_type=MESH)

    def is_self(t):
        return (u * nblk + t // nsub == r) & (lax.rem(t, nsub) == u)

    def send_grad(k, carry):
        t = lax.rem(k + me, nres)

        @pl.when(jnp.logical_not(is_self(t)))
        def _():
            grad_copy(r, t).start()

        @pl.when(is_self(t))
        def _():
            drecv[r] = dstage[t]

        return carry

    lax.fori_loop(0, nres, send_grad, 0)

    bt = [bmat[half, :, 0:256].astype(f32).T.astype(bf16) for half in range(2)]

    for p in range(8):
        g = gmat[:, p * 256:(p + 1) * 256]
        for half in range(2):
            part = dot(bt[half], g)
            for d in range(32):
                rows = part[d * 8:(d + 1) * 8, :]
                pair_rows = jnp.concatenate([rows[:, :128], rows[:, 128:]], axis=0)
                dmat[half, p * 16:(p + 1) * 16, d * 128:(d + 1) * 128] = pair_rows.astype(bf16)

    at_mine = mine_left.T[0:32].astype(bf16)
    at_other = other_left.T[0:32].astype(bf16)
    for q in range(8):
        lanes = slice(q * 512, (q + 1) * 512)
        part = dot(at_mine, dmat[u, :, lanes]) + dot(at_other, dmat[1 - u, :, lanes])
        for k in range(4):
            d = q * 4 + k
            rows = slice(d // near * 32, d // near * 32 + 32)
            ostage[d % near, rows, :] = part[:, k * 128:(k + 1) * 128].astype(bf16)

    def near_copy(dst, src):
        return pltpu.make_async_remote_copy(
            src_ref=ostage.at[dst], dst_ref=orecv.at[src], send_sem=osend.at[dst], recv_sem=orecv_sem.at[src],
            device_id=place(layer * near + dst), device_id_type=MESH)

    def far_copy(dst, src):
        return pltpu.make_async_remote_copy(
            src_ref=fstage.at[dst], dst_ref=frecv.at[src], send_sem=fsend.at[dst], recv_sem=frecv_sem.at[src],
            device_id=place(dst * near + spot), device_id_type=MESH)

    def far_gather(dst, src):
        rows = pl.ds(pl.multiple_of(src * 32, 32), 32)
        return pltpu.make_async_remote_copy(
            src_ref=owned, dst_ref=ogather.at[spot, rows, :], send_sem=hsend.at[dst], recv_sem=hrecv.at[src],
            device_id=place(dst * near + spot), device_id_type=MESH)

    def near_gather(dst, src):
        return pltpu.make_async_remote_copy(
            src_ref=ogather.at[spot], dst_ref=ogather.at[src], send_sem=gsend.at[dst], recv_sem=grecv.at[src],
            device_id=place(layer * near + dst), device_id_type=MESH)

    for k in range(1, near):
        near_copy(lax.rem(spot + k, near), spot).start()
    orecv[spot] = ostage[spot]

    da_send[...] = dot(dmat[1 - u], wm[...], ((1,), (1,)))

    def da_copy():
        return pltpu.make_async_remote_copy(
            src_ref=da_send, dst_ref=da_recv, send_sem=psend.at[1], recv_sem=precv.at[1],
            device_id={"res": r, "sub": 1 - u}, device_id_type=MESH)

    da_copy().start()
    da = dot(dmat[u], wm[...], ((1,), (1,)))

    for p in range(8):
        lanes = slice(p * 256, (p + 1) * 256)
        z = dot(bmat[0, :, 0:256], tmat[0, :, lanes]) + dot(bmat[1, :, 0:256], tmat[1, :, lanes])
        for k in range(2):
            i = p * 2 + k
            pair[i] = ((z[:, k * 128:(k + 1) * 128] + offset[...]) * scale[:, i:i + 1]).astype(bf16)

    outs[0].start()
    for k in range(1, near):
        near_copy(0, lax.rem(spot + k, near)).wait_recv()
    near_total = orecv[0].astype(f32)
    for k in range(1, near):
        near_total = near_total + orecv[k].astype(f32)
    for k in range(far):
        fstage[k] = near_total[k * 32:(k + 1) * 32].astype(bf16)
    for k in range(1, far):
        far_copy(lax.rem(layer + k, far), layer).start()
    frecv[layer] = fstage[layer]

    da_copy().wait()

    def wait_grad(k, carry):
        @pl.when((k != r) | (home != u))
        def _():
            grad_copy(k, 0).wait_recv()

        return carry

    lax.fori_loop(0, nres, wait_grad, 0)
    total = drecv[0].astype(f32)
    for k in range(1, nres):
        total = total + drecv[k].astype(f32)
    highest = lax.Precision.HIGHEST
    wide_rows = dot(onehot((128, 16), lambda a, b: a // 8 == b), total, precision=highest) * keep[:, :256]
    db_rows = dot(wide_rows, onehot((256, 128), lambda a, b: b % 64 == 32 + a // 8), precision=highest)
    dfeat = ((da + da_recv[...] + db_rows) * mask).astype(bf16)
    twice = dot(normed16, onehot((64, 128), lambda a, b: b % 64 == a).astype(bf16)).astype(bf16)
    grads = dot(dfeat, twice, ((0,), (0,)))
    low = lax.broadcasted_iota(jnp.int32, (32, 128), 1) < 64
    small[0:32] = jnp.where(low, grads[0:32], grads[32:64]).astype(bf16)
    small[32:48] = jnp.broadcast_to(bias, (16, 128)).astype(bf16)

    def small_copy(dst, src):
        return pltpu.make_async_remote_copy(
            src_ref=small, dst_ref=small_recv.at[src], send_sem=wsend.at[dst], recv_sem=wrecv.at[src],
            device_id=place(layer * near + dst), device_id_type=MESH)

    def plane_copy(dst, src):
        return pltpu.make_async_remote_copy(
            src_ref=plane, dst_ref=plane_recv.at[src], send_sem=vsend.at[dst], recv_sem=vrecv.at[src],
            device_id=place(dst * near + spot), device_id_type=MESH)

    for k in range(1, near):
        small_copy(lax.rem(spot + k, near), spot).start()
    small_recv[spot] = small[...]

    for k in range(1, far):
        far_copy(0, lax.rem(layer + k, far)).wait_recv()
    far_total = frecv[0].astype(f32)
    for k in range(1, far):
        far_total = far_total + frecv[k].astype(f32)
    owned[...] = far_total.astype(bf16)
    for k in range(1, far):
        far_gather(lax.rem(layer + k, far), layer).start()
    ogather[spot, pl.ds(pl.multiple_of(layer * 32, 32), 32), :] = far_total.astype(bf16)

    for k in range(1, near):
        small_copy(0, lax.rem(spot + k, near)).wait_recv()
    near_sum = small_recv[0].astype(f32)
    for k in range(1, near):
        near_sum = near_sum + small_recv[k].astype(f32)
    plane[...] = near_sum.astype(bf16)
    for k in range(1, far):
        plane_copy(lax.rem(layer + k, far), layer).start()
    plane_recv[layer] = plane[...]

    for k in range(1, far):
        far_gather(0, lax.rem(layer + k, far)).wait_recv()
    for k in range(1, near):
        near_gather(lax.rem(spot + k, near), spot).start()

    dnormed = dot(dfeat, wab_t)
    rows_out[...] = inv_std * (
        dnormed - jnp.mean(dnormed, axis=-1, keepdims=True)
        - normed * jnp.mean(dnormed * normed, axis=-1, keepdims=True))
    for s in range(8):
        align[s] = rows_out[pl.ds(s, 16, stride=8), :]

    outs[1].start()
    for k in range(1, far):
        plane_copy(0, lax.rem(layer + k, far)).wait_recv()
    inv = 1.0 / (16 * nres)
    sums = plane_recv[0].astype(f32)
    for k in range(1, far):
        sums = sums + plane_recv[k].astype(f32)
    sums = sums * inv
    wa_out[...] = sums[0:32, 0:64]
    wb_out[...] = sums[0:32, 64:128]
    bias_out[...] = sums[32:33]
    for copy in (outs[2], outs[3], outs[5]):
        copy.start()

    for k in range(1, near):
        near_gather(0, lax.rem(spot + k, near)).wait_recv()
    for d in range(32):
        lin_out[pl.ds(d, 32, stride=32), :] = ogather[d % near, d // near * 32:d // near * 32 + 32, :].astype(f32) * inv
    outs[4].start()

    for k in range(1, near):
        small_copy(lax.rem(spot + k, near), spot).wait_send()
        near_copy(lax.rem(spot + k, near), spot).wait_send()
        near_gather(lax.rem(spot + k, near), spot).wait_send()
    for k in range(1, far):
        plane_copy(lax.rem(layer + k, far), layer).wait_send()
        far_copy(lax.rem(layer + k, far), layer).wait_send()
        far_gather(lax.rem(layer + k, far), layer).wait_send()

    def drain_near(k, carry):
        @pl.when((k != 0) | (home != u))
        def _():
            block_copy(k).wait_send()

        @pl.when(jnp.logical_not(is_self(k)))
        def _():
            grad_copy(r, k).wait_send()

        return carry

    lax.fori_loop(0, nres, drain_near, 0)
    for copy in outs:
        copy.wait()


def hand_over(*refs):
    count = (len(refs) - 2) // 3
    take, give = refs[-2], refs[-1]
    held = refs[2 * count:3 * count]
    first = [pltpu.make_async_copy(refs[k], held[k], take.at[k]) for k in range(count)]
    second = [pltpu.make_async_copy(held[k], refs[count + k], give.at[k]) for k in range(count)]
    for copy in first:
        copy.start()
    for k in range(count):
        first[k].wait()
        second[k].start()
    for copy in second:
        copy.wait()


def fused(
    nres, nsub,
    sequence_embedding,
    sequence_present_flags,
    position_couple_flags,
    first_factor_matrix,
    second_factor_matrix,
    final_linear_matrix,
    final_offset_vector,
    couple_change_cotangent,
):
    bf16, f32 = jnp.bfloat16, jnp.float32
    n = nres * nsub
    anywhere = pl.BlockSpec(memory_space=pl.ANY)
    dma = pltpu.SemaphoreType.DMA
    shapes = (
        jax.ShapeDtypeStruct((16, 128, 128), bf16),
        jax.ShapeDtypeStruct((8, 16, 64), f32),
        jax.ShapeDtypeStruct((32, 64), f32),
        jax.ShapeDtypeStruct((32, 64), f32),
        jax.ShapeDtypeStruct((1024, 128), f32),
        jax.ShapeDtypeStruct((1, 128), f32),
    )
    operands = (
        sequence_embedding, sequence_present_flags, position_couple_flags,
        first_factor_matrix.T, second_factor_matrix.T,
        final_linear_matrix, final_offset_vector.reshape(1, 128), couple_change_cotangent,
    )
    outs = pl.pallas_call(
        functools.partial(kernel, nres, nsub),
        out_shape=shapes,
        in_specs=[anywhere] * 8,
        out_specs=(anywhere,) * 6,
        scratch_shapes=[pltpu.VMEM(a.shape, a.dtype) for a in operands + shapes] + [
            pltpu.VMEM((128, 128), bf16),
            pltpu.VMEM((128, 128), bf16),
            pltpu.VMEM((16, 384), bf16),
            pltpu.VMEM((2, 128, 384), bf16),
            pltpu.VMEM((128, 4096), bf16),
            pltpu.VMEM((1024, 128), f32),
            pltpu.VMEM((2, 256, 2048), bf16),
            pltpu.VMEM((128, 2048), bf16),
            pltpu.VMEM((2, 128, 4096), bf16),
            pltpu.VMEM((nres, 16, 256), bf16),
            pltpu.VMEM((nres, 16, 256), bf16),
            pltpu.VMEM((8, n * 4, 128), bf16),
            pltpu.VMEM((8, n * 4, 128), bf16),
            pltpu.VMEM((8, n * 4, 128), bf16),
            pltpu.VMEM((n // 8, 32, 128), bf16),
            pltpu.VMEM((n // 8, 32, 128), bf16),
            pltpu.VMEM((32, 128), bf16),
            pltpu.VMEM((128, 128), f32),
            pltpu.VMEM((128, 128), f32),
            pltpu.VMEM((48, 128), bf16),
            pltpu.VMEM((8, 48, 128), bf16),
            pltpu.VMEM((48, 128), bf16),
            pltpu.VMEM((n // 8, 48, 128), bf16),
            pltpu.VMEM((128, 64), f32),
            dma((8,)), dma((6,)),
            dma((nres,)), dma((nres,)),
            dma((nres,)), dma((nres,)),
            dma((8,)), dma((8,)),
            dma((8,)), dma((8,)),
            dma((8,)), dma((8,)),
            dma((2,)), dma((2,)),
            dma((n // 8,)), dma((n // 8,)),
            dma((n // 8,)), dma((n // 8,)),
            dma((n // 8,)), dma((n // 8,)),
        ],
        compiler_params=pltpu.CompilerParams(
            collective_id=0, has_side_effects=True, vmem_limit_bytes=60 * 1024 * 1024
        ),
    )(*operands)
    outs = pl.pallas_call(
        hand_over,
        out_shape=shapes,
        in_specs=[anywhere] * 6,
        out_specs=(anywhere,) * 6,
        scratch_shapes=[pltpu.VMEM(a.shape, a.dtype) for a in shapes] + [dma((6,)), dma((6,))],
        compiler_params=pltpu.CompilerParams(vmem_limit_bytes=60 * 1024 * 1024),
    )(*outs)
    return (outs[0], outs[1], outs[2].T, outs[3].T, outs[4], outs[5].reshape(128))


def body(
    sequence_embedding,
    sequence_present_flags,
    position_couple_flags,
    first_factor_matrix,
    second_factor_matrix,
    final_linear_matrix,
    final_offset_vector,
    couple_change_cotangent,
):
    highest = lax.Precision.HIGHEST
    precise_scalar = jnp.float32
    hidden = first_factor_matrix.shape[1]
    pair_width = final_linear_matrix.shape[1]
    position_span = sequence_embedding.shape[1]
    col_width = couple_change_cotangent.shape[1]
    col_start = lax.axis_index("sub") * col_width
    present_count_items = sequence_embedding.astype(precise_scalar)
    centred = present_count_items - jnp.mean(present_count_items, axis=-1, keepdims=True)
    variance = jnp.mean(centred * centred, axis=-1, keepdims=True)
    reciprocal_deviation = lax.rsqrt(variance + 1e-05)
    normalized_input = centred * reciprocal_deviation
    layer_scaled_half = normalized_input.astype(jnp.bfloat16)
    row_presence_mask = sequence_present_flags.astype(precise_scalar)[:, None, :]
    first_factor_features = jnp.einsum(
        "sim,mc->sci", layer_scaled_half, first_factor_matrix, preferred_element_type=precise_scalar
    )
    second_factor_features = jnp.einsum(
        "sim,mc->sci",
        layer_scaled_half,
        second_factor_matrix,
        preferred_element_type=precise_scalar,
    )
    feat_a = (first_factor_features * row_presence_mask).astype(jnp.bfloat16)
    feat_b = (second_factor_features * row_presence_mask).astype(jnp.bfloat16)
    mask16 = row_presence_mask.astype(jnp.bfloat16)
    all_a, all_b, all_mask = (
        lax.all_gather(feat_a, "sub", axis=0, tiled=True),
        lax.all_gather(feat_b, "sub", axis=0, tiled=True),
        lax.all_gather(mask16, "sub", axis=0, tiled=True),
    )
    wide_b, wide_mask = (
        lax.all_gather(all_b, "res", axis=2, tiled=True),
        lax.all_gather(all_mask, "res", axis=2, tiled=True),
    )
    col_b = lax.dynamic_slice_in_dim(wide_b, col_start, col_width, 2)
    col_mask = lax.dynamic_slice_in_dim(wide_mask, col_start, col_width, 2)
    pair_count = jnp.einsum(
        "sxi,sxj->ij", all_mask, col_mask, preferred_element_type=precise_scalar
    )
    divisor = jnp.maximum(pair_count, 1.0)[:, :, None]
    out_cube = final_linear_matrix.reshape(hidden, hidden, pair_width)
    tmix = jnp.einsum(
        "sci,cde->side", all_a, out_cube, preferred_element_type=precise_scalar
    ).astype(jnp.bfloat16)
    zsum = jnp.einsum("side,sdj->ije", tmix, col_b, preferred_element_type=precise_scalar)
    pmask = position_couple_flags.astype(precise_scalar)[:, :, None]
    pair_delta_output = (pmask * (zsum + final_offset_vector) / divisor).astype(jnp.bfloat16)
    gscaled32 = couple_change_cotangent * pmask / divisor
    bias_part = jnp.sum(gscaled32, axis=(0, 1))
    gscaled = gscaled32.astype(jnp.bfloat16)
    dtmix = jnp.einsum("ije,sdj->side", gscaled, col_b, preferred_element_type=precise_scalar)
    db_part = jnp.einsum("ije,side->sdj", gscaled, tmix, preferred_element_type=precise_scalar)
    cube_f32 = out_cube.astype(precise_scalar)
    da_part = jnp.einsum("side,cde->sci", dtmix, cube_f32, precision=highest)
    out_part = jnp.einsum("sci,side->cde", all_a.astype(precise_scalar), dtmix, precision=highest)
    placed = jnp.zeros((db_part.shape[0], hidden, wide_b.shape[2]), precise_scalar)
    placed = lax.dynamic_update_slice_in_dim(placed, db_part, col_start, 2)
    res_totals = lax.psum_scatter(placed, "res", scatter_dimension=2, tiled=True)
    da_rows, db_rows = (
        lax.psum_scatter(da_part, "sub", scatter_dimension=0, tiled=True),
        lax.psum_scatter(res_totals, "sub", scatter_dimension=0, tiled=True),
    )
    dfeat_a = da_rows * row_presence_mask
    dfeat_b = db_rows * row_presence_mask
    normed_f = layer_scaled_half.astype(precise_scalar)
    wa_part = jnp.einsum("sim,sci->mc", normed_f, dfeat_a, precision=highest)
    wb_part = jnp.einsum("sim,sci->mc", normed_f, dfeat_b, precision=highest)
    totals = lax.psum((out_part, bias_part, wa_part, wb_part), ("res", "sub"))
    inv_res = 1.0 / (position_span * lax.axis_size("res"))
    output_weight_gradient = totals[0].reshape(hidden * hidden, pair_width) * inv_res
    output_bias_gradient = totals[1] * inv_res
    left_weight_gradient = totals[2] * inv_res
    right_weight_gradient = totals[3] * inv_res
    normalized_gradient = jnp.einsum(
        "sci,mc->sim", dfeat_a, first_factor_matrix.astype(precise_scalar), precision=highest
    )
    normalized_gradient = normalized_gradient + jnp.einsum(
        "sci,mc->sim", dfeat_b, second_factor_matrix.astype(precise_scalar), precision=highest
    )
    alignment_gradient = reciprocal_deviation * (
        normalized_gradient
        - jnp.mean(normalized_gradient, axis=-1, keepdims=True)
        - normalized_input
        * jnp.mean(normalized_gradient * normalized_input, axis=-1, keepdims=True)
    )
    return (
        pair_delta_output,
        alignment_gradient,
        left_weight_gradient,
        right_weight_gradient,
        output_weight_gradient,
        output_bias_gradient,
    )


def solution(mesh):
    in_specs = (
        P("sub", ("groups", "res"), None),
        P("sub", ("groups", "res")),
        P(("groups", "res"), "sub"),
        P(),
        P(),
        P(),
        P(),
        P(("groups", "res"), "sub", None),
    )
    out_specs = (
        P(("groups", "res"), "sub", None),
        P("sub", ("groups", "res"), None),
        P("groups", None),
        P("groups", None),
        P("groups", None),
        P("groups"),
    )
    nres, nsub = mesh.shape["res"], mesh.shape["sub"]
    chosen = functools.partial(fused, nres, nsub) if (nres, nsub) == (16, 2) else body
    return jax.shard_map(chosen, mesh=mesh, in_specs=in_specs, out_specs=out_specs, check_vma=False)
```

```python
import functools

import jax
import jax.numpy as jnp
from jax import lax
from jax.sharding import PartitionSpec as P
from jax.experimental import pallas as pl
from jax.experimental.pallas import tpu as pltpu


MESH = pl.DeviceIdType.MESH


def onehot(shape, test):
    rows = lax.broadcasted_iota(jnp.int32, shape, 0)
    lanes = lax.broadcasted_iota(jnp.int32, shape, 1)
    return jnp.where(test(rows, lanes), 1.0, 0.0)


def dot(a, b, dims=((1,), (0,)), precision=None):
    return lax.dot_general(a, b, (dims, ((), ())), preferred_element_type=jnp.float32, precision=precision)


def kernel(
    nres, nsub,
    emb_hbm, flags_hbm, pflags_hbm, wa_hbm, wb_hbm, lin_hbm, offset_hbm, cot_hbm,
    pair_hbm, align_hbm, wa_hbm_out, wb_hbm_out, lin_hbm_out, bias_hbm_out,
    emb, flags, pflags, wa_t, wb_t, lin, offset, cot,
    pair, align, wa_out, wb_out, lin_out, bias_out, feat, other, blk, bmat, wm, lin32, tmat, gmat, dmat, dstage, drecv,
    ostage, orecv, ogather, fstage, frecv, owned, da_send, da_recv, small, small_recv, plane, plane_recv, rows_out,
    in_sem, out_sem, bsend, brecv, dsend, drecv_sem, osend, orecv_sem, gsend, grecv, wsend, wrecv, psend, precv, vsend, vrecv, fsend, frecv_sem, hsend, hrecv,
):
    bf16, f32 = jnp.bfloat16, jnp.float32
    n = nres * nsub
    nblk = nres // nsub
    r, u = lax.axis_index("res"), lax.axis_index("sub")
    me = r * nsub + u

    def place(k):
        return {"res": k // nsub, "sub": lax.rem(k, nsub)}

    ins = [
        pltpu.make_async_copy(a, b, in_sem.at[k])
        for k, (a, b) in enumerate([
            (emb_hbm, emb), (flags_hbm, flags), (wa_hbm, wa_t), (wb_hbm, wb_t),
            (lin_hbm, lin), (pflags_hbm, pflags), (offset_hbm, offset), (cot_hbm, cot)])
    ]
    outs = [
        pltpu.make_async_copy(a, b, out_sem.at[k])
        for k, (a, b) in enumerate([
            (pair, pair_hbm), (align, align_hbm), (wa_out, wa_hbm_out),
            (wb_out, wb_hbm_out), (lin_out, lin_hbm_out), (bias_out, bias_hbm_out)])
    ]
    for copy in ins:
        copy.start()
    near = 8
    far = n // near
    spot, layer = lax.rem(me, near), me // near
    barrier = pltpu.get_barrier_semaphore()

    def greet(k, carry):
        pl.semaphore_signal(barrier, inc=1, device_id=place(lax.rem(me + k, n)), device_id_type=MESH)
        return carry

    lax.fori_loop(1, n, greet, 0)

    for copy in ins[:4]:
        copy.wait()
    wab_t = jnp.concatenate([wa_t[...], wb_t[...], jnp.zeros((64, 64), bf16)], axis=0)

    x = dot(onehot((128, 128), lambda a, b: b == (a % 8) * 16 + a // 8).astype(bf16), emb[...].reshape(128, 64))
    centred = x - jnp.mean(x, axis=-1, keepdims=True)
    inv_std = lax.rsqrt(jnp.mean(centred * centred, axis=-1, keepdims=True) + 1e-05)
    normed = centred * inv_std
    normed16 = normed.astype(bf16)
    picked = dot(onehot((128, 8), lambda a, b: a % 8 == b).astype(bf16), flags[...].astype(f32).astype(bf16))
    mask = jnp.sum(picked * onehot((128, 16), lambda a, b: a // 8 == b), axis=1, keepdims=True)
    projected = dot(normed16, wab_t, ((1,), (1,))) * mask
    projected = projected + mask * onehot((128, 128), lambda a, b: b - 64 == a % 8)
    feat[...] = projected.astype(bf16)
    keep = onehot((128, 384), lambda a, b: a % 8 == b % 8)
    spread = onehot((128, 384), lambda a, b: ((b < 256) & (a == 32 + b // 8)) | ((a >= 64) & (b - 256 == a)))
    gather_rows = onehot((16, 128), lambda a, b: a == b // 8).astype(bf16)
    mine = dot(gather_rows, (dot(feat[...], spread.astype(bf16)) * keep).astype(bf16)).astype(bf16)
    blk[...] = mine
    home = r // nblk
    slot = u * nblk + lax.rem(r, nblk)
    rows_here = pl.ds(pl.multiple_of(lax.rem(r, nblk) * 16, 16), 16)

    pl.semaphore_wait(barrier, n - 1)

    def partner_copy():
        return pltpu.make_async_remote_copy(
            src_ref=feat, dst_ref=other, send_sem=psend.at[0], recv_sem=precv.at[0],
            device_id={"res": r, "sub": 1 - u}, device_id_type=MESH)

    partner_copy().start()

    core = lax.rem(r, 2)
    chips = nres // 2
    spot_in = lax.rem(r, nblk) // 2

    def block_copy(k):
        q = lax.rem(r // 2 + k, chips) * 2 + core
        return pltpu.make_async_remote_copy(
            src_ref=blk, dst_ref=bmat.at[u, spot_in, core], send_sem=bsend.at[k], recv_sem=brecv.at[slot // 2],
            device_id={"res": q, "sub": home}, device_id_type=MESH)

    def pass_copy(which):
        return pltpu.make_async_remote_copy(
            src_ref=bmat.at[:, :, core], dst_ref=bmat.at[:, :, which], send_sem=bsend.at[chips], recv_sem=brecv.at[chips],
            device_id={"res": r // 2 * 2 + 1 - core, "sub": u}, device_id_type=MESH)

    for k in range(1, chips):
        block_copy(k).start()

    @pl.when(home != u)
    def _():
        block_copy(0).start()

    @pl.when(home == u)
    def _():
        bmat[u, spot_in, core] = mine

    ins[4].wait()
    lin32[...] = lin[...].astype(f32)
    wm[...] = jnp.zeros_like(wm)
    for d in range(32):
        piece = lin32[pl.ds(d, 32, stride=32), :].astype(bf16)
        wm[0:32, d * 128:(d + 1) * 128] = piece
        wm[64:96, d * 128:(d + 1) * 128] = piece

    lane128 = lax.broadcasted_iota(jnp.int32, (128, 128), 1)

    def left_only(ref):
        return jnp.where(lane128 < 32, ref[...].astype(f32), 0.0)

    def mix(half, left):
        for p in range(16):
            part = dot(left, wm[:, p * 256:(p + 1) * 256])
            for i in range(16):
                rows = part[i * 8:(i + 1) * 8, :]
                pair_rows = jnp.concatenate([rows[:, :128], rows[:, 128:]], axis=0)
                tmat[half, p * 16:(p + 1) * 16, i * 128:(i + 1) * 128] = pair_rows.astype(bf16)

    mine_left = left_only(feat)
    mix(u, mine_left.astype(bf16))
    partner_copy().wait()
    for k in range(chips):
        copy = pltpu.make_async_remote_copy(
            src_ref=blk, dst_ref=bmat.at[k // (nblk // 2), k % (nblk // 2), core], send_sem=bsend.at[0],
            recv_sem=brecv.at[k], device_id={"res": r, "sub": 1 - u}, device_id_type=MESH)

        @pl.when((slot // 2 != k) | (home != u))
        def _():
            copy.wait_recv()

    pass_copy(core).start()
    other_left = left_only(other)
    mix(1 - u, other_left.astype(bf16))

    mask_rows = [dot(gather_rows, ref[...]).astype(bf16) for ref in (feat, other)]

    for copy in ins[5:]:
        copy.wait()

    pass_copy(1 - core).wait_recv()

    def cols(half):
        return bmat[half].reshape(128, 384)

    count = dot(mask_rows[0], cols(u)[:, 256:384], ((1,), (1,))) + dot(mask_rows[1], cols(1 - u)[:, 256:384], ((1,), (1,)))
    scale = (pflags[...].astype(f32) / jnp.maximum(count, 1.0)).T
    bias = jnp.zeros((1, 128), f32)
    for i in range(16):
        g32 = cot[i] * scale[:, i:i + 1]
        bias = bias + jnp.sum(g32, axis=0, keepdims=True)
        gmat[:, i * 128:(i + 1) * 128] = g32.astype(bf16)

    for half in range(2):
        db = dot(gmat[...], tmat[half], ((1,), (1,))).astype(bf16)
        for k in range(nblk):
            dstage[k * 2 + half] = db[k * 16:(k + 1) * 16, :]

    def grad_copy(k, t):
        return pltpu.make_async_remote_copy(
            src_ref=dstage.at[t], dst_ref=drecv.at[r], send_sem=dsend.at[t], recv_sem=drecv_sem.at[k],
            device_id={"res": u * nblk + t // nsub, "sub": lax.rem(t, nsub)}, device_id_type=MESH)

    def is_self(t):
        return (u * nblk + t // nsub == r) & (lax.rem(t, nsub) == u)

    def send_grad(k, carry):
        t = lax.rem(k + me, nres)

        @pl.when(jnp.logical_not(is_self(t)))
        def _():
            grad_copy(r, t).start()

        @pl.when(is_self(t))
        def _():
            drecv[r] = dstage[t]

        return carry

    lax.fori_loop(0, nres, send_grad, 0)

    bt = [cols(half)[:, 0:256].astype(f32).T.astype(bf16) for half in range(2)]

    for p in range(8):
        g = gmat[:, p * 256:(p + 1) * 256]
        for half in range(2):
            part = dot(bt[half], g)
            for d in range(32):
                rows = part[d * 8:(d + 1) * 8, :]
                pair_rows = jnp.concatenate([rows[:, :128], rows[:, 128:]], axis=0)
                dmat[half, p * 16:(p + 1) * 16, d * 128:(d + 1) * 128] = pair_rows.astype(bf16)

    at_mine = mine_left.T[0:32].astype(bf16)
    at_other = other_left.T[0:32].astype(bf16)
    for q in range(8):
        lanes = slice(q * 512, (q + 1) * 512)
        part = dot(at_mine, dmat[u, :, lanes]) + dot(at_other, dmat[1 - u, :, lanes])
        for k in range(4):
            d = q * 4 + k
            rows = slice(d // near * 32, d // near * 32 + 32)
            ostage[d % near, rows, :] = part[:, k * 128:(k + 1) * 128].astype(bf16)

    def near_copy(dst, src):
        return pltpu.make_async_remote_copy(
            src_ref=ostage.at[dst], dst_ref=orecv.at[src], send_sem=osend.at[dst], recv_sem=orecv_sem.at[src],
            device_id=place(layer * near + dst), device_id_type=MESH)

    def far_copy(dst, src):
        return pltpu.make_async_remote_copy(
            src_ref=fstage.at[dst], dst_ref=frecv.at[src], send_sem=fsend.at[dst], recv_sem=frecv_sem.at[src],
            device_id=place(dst * near + spot), device_id_type=MESH)

    def far_gather(dst, src):
        rows = pl.ds(pl.multiple_of(src * 32, 32), 32)
        return pltpu.make_async_remote_copy(
            src_ref=owned, dst_ref=ogather.at[spot, rows, :], send_sem=hsend.at[dst], recv_sem=hrecv.at[src],
            device_id=place(dst * near + spot), device_id_type=MESH)

    def near_gather(dst, src):
        return pltpu.make_async_remote_copy(
            src_ref=ogather.at[spot], dst_ref=ogather.at[src], send_sem=gsend.at[dst], recv_sem=grecv.at[src],
            device_id=place(layer * near + dst), device_id_type=MESH)

    for k in range(1, near):
        near_copy(lax.rem(spot + k, near), spot).start()
    orecv[spot] = ostage[spot]

    da_send[...] = dot(dmat[1 - u], wm[...], ((1,), (1,))).astype(bf16)

    def da_copy():
        return pltpu.make_async_remote_copy(
            src_ref=da_send, dst_ref=da_recv, send_sem=psend.at[1], recv_sem=precv.at[1],
            device_id={"res": r, "sub": 1 - u}, device_id_type=MESH)

    da_copy().start()
    da = dot(dmat[u], wm[...], ((1,), (1,)))

    for p in range(8):
        lanes = slice(p * 256, (p + 1) * 256)
        z = dot(cols(0)[:, 0:256], tmat[0, :, lanes]) + dot(cols(1)[:, 0:256], tmat[1, :, lanes])
        for k in range(2):
            i = p * 2 + k
            pair[i] = ((z[:, k * 128:(k + 1) * 128] + offset[...]) * scale[:, i:i + 1]).astype(bf16)

    outs[0].start()
    for k in range(1, near):
        near_copy(0, lax.rem(spot + k, near)).wait_recv()
    near_total = orecv[0].astype(f32)
    for k in range(1, near):
        near_total = near_total + orecv[k].astype(f32)
    for k in range(far):
        fstage[k] = near_total[k * 32:(k + 1) * 32].astype(bf16)
    for k in range(1, far):
        far_copy(lax.rem(layer + k, far), layer).start()
    frecv[layer] = fstage[layer]

    da_copy().wait()

    def wait_grad(k, carry):
        @pl.when((k != r) | (home != u))
        def _():
            grad_copy(k, 0).wait_recv()

        return carry

    lax.fori_loop(0, nres, wait_grad, 0)
    total = drecv[0].astype(f32)
    for k in range(1, nres):
        total = total + drecv[k].astype(f32)
    highest = lax.Precision.HIGHEST
    wide_rows = dot(onehot((128, 16), lambda a, b: a // 8 == b), total, precision=highest) * keep[:, :256]
    db_rows = dot(wide_rows, onehot((256, 128), lambda a, b: b % 64 == 32 + a // 8), precision=highest)
    dfeat = ((da + da_recv[...].astype(f32) + db_rows) * mask).astype(bf16)
    twice = dot(normed16, onehot((64, 128), lambda a, b: b % 64 == a).astype(bf16)).astype(bf16)
    grads = dot(dfeat, twice, ((0,), (0,)))
    low = lax.broadcasted_iota(jnp.int32, (32, 128), 1) < 64
    small[0:32] = jnp.where(low, grads[0:32], grads[32:64]).astype(bf16)
    small[32:48] = jnp.broadcast_to(bias, (16, 128)).astype(bf16)

    def small_copy(dst, src):
        return pltpu.make_async_remote_copy(
            src_ref=small, dst_ref=small_recv.at[src], send_sem=wsend.at[dst], recv_sem=wrecv.at[src],
            device_id=place(layer * near + dst), device_id_type=MESH)

    def plane_copy(dst, src):
        return pltpu.make_async_remote_copy(
            src_ref=plane, dst_ref=plane_recv.at[src], send_sem=vsend.at[dst], recv_sem=vrecv.at[src],
            device_id=place(dst * near + spot), device_id_type=MESH)

    for k in range(1, near):
        small_copy(lax.rem(spot + k, near), spot).start()
    small_recv[spot] = small[...]

    for k in range(1, far):
        far_copy(0, lax.rem(layer + k, far)).wait_recv()
    far_total = frecv[0].astype(f32)
    for k in range(1, far):
        far_total = far_total + frecv[k].astype(f32)
    owned[...] = far_total.astype(bf16)
    for k in range(1, far):
        far_gather(lax.rem(layer + k, far), layer).start()
    ogather[spot, pl.ds(pl.multiple_of(layer * 32, 32), 32), :] = far_total.astype(bf16)

    for k in range(1, near):
        small_copy(0, lax.rem(spot + k, near)).wait_recv()
    near_sum = small_recv[0].astype(f32)
    for k in range(1, near):
        near_sum = near_sum + small_recv[k].astype(f32)
    plane[...] = near_sum.astype(bf16)
    for k in range(1, far):
        plane_copy(lax.rem(layer + k, far), layer).start()
    plane_recv[layer] = plane[...]

    for k in range(1, far):
        far_gather(0, lax.rem(layer + k, far)).wait_recv()
    for k in range(1, near):
        near_gather(lax.rem(spot + k, near), spot).start()

    dnormed = dot(dfeat, wab_t)
    rows_out[...] = inv_std * (
        dnormed - jnp.mean(dnormed, axis=-1, keepdims=True)
        - normed * jnp.mean(dnormed * normed, axis=-1, keepdims=True))
    for s in range(8):
        align[s] = rows_out[pl.ds(s, 16, stride=8), :]

    outs[1].start()
    for k in range(1, far):
        plane_copy(0, lax.rem(layer + k, far)).wait_recv()
    inv = 1.0 / (16 * nres)
    sums = plane_recv[0].astype(f32)
    for k in range(1, far):
        sums = sums + plane_recv[k].astype(f32)
    sums = sums * inv
    wa_out[...] = sums[0:32, 0:64]
    wb_out[...] = sums[0:32, 64:128]
    bias_out[...] = sums[32:33]
    for copy in (outs[2], outs[3], outs[5]):
        copy.start()

    for k in range(1, near):
        near_gather(0, lax.rem(spot + k, near)).wait_recv()
    for d in range(32):
        lin_out[pl.ds(d, 32, stride=32), :] = ogather[d % near, d // near * 32:d // near * 32 + 32, :].astype(f32) * inv
    outs[4].start()

    for k in range(1, near):
        small_copy(lax.rem(spot + k, near), spot).wait_send()
        near_copy(lax.rem(spot + k, near), spot).wait_send()
        near_gather(lax.rem(spot + k, near), spot).wait_send()
    for k in range(1, far):
        plane_copy(lax.rem(layer + k, far), layer).wait_send()
        far_copy(lax.rem(layer + k, far), layer).wait_send()
        far_gather(lax.rem(layer + k, far), layer).wait_send()

    def drain_near(k, carry):
        @pl.when(jnp.logical_not(is_self(k)))
        def _():
            grad_copy(r, k).wait_send()

        return carry

    lax.fori_loop(0, nres, drain_near, 0)
    for k in range(1, chips):
        block_copy(k).wait_send()

    @pl.when(home != u)
    def _():
        block_copy(0).wait_send()

    pass_copy(core).wait_send()
    for copy in outs:
        copy.wait()


def hand_over(*refs):
    count = (len(refs) - 2) // 3
    take, give = refs[-2], refs[-1]
    held = refs[2 * count:3 * count]
    first = [pltpu.make_async_copy(refs[k], held[k], take.at[k]) for k in range(count)]
    second = [pltpu.make_async_copy(held[k], refs[count + k], give.at[k]) for k in range(count)]
    for copy in first:
        copy.start()
    for k in range(count):
        first[k].wait()
        second[k].start()
    for copy in second:
        copy.wait()


def fused(
    nres, nsub,
    sequence_embedding,
    sequence_present_flags,
    position_couple_flags,
    first_factor_matrix,
    second_factor_matrix,
    final_linear_matrix,
    final_offset_vector,
    couple_change_cotangent,
):
    bf16, f32 = jnp.bfloat16, jnp.float32
    n = nres * nsub
    anywhere = pl.BlockSpec(memory_space=pl.ANY)
    dma = pltpu.SemaphoreType.DMA
    shapes = (
        jax.ShapeDtypeStruct((16, 128, 128), bf16),
        jax.ShapeDtypeStruct((8, 16, 64), f32),
        jax.ShapeDtypeStruct((32, 64), f32),
        jax.ShapeDtypeStruct((32, 64), f32),
        jax.ShapeDtypeStruct((1024, 128), f32),
        jax.ShapeDtypeStruct((1, 128), f32),
    )
    operands = (
        sequence_embedding, sequence_present_flags, position_couple_flags,
        first_factor_matrix.T, second_factor_matrix.T,
        final_linear_matrix, final_offset_vector.reshape(1, 128), couple_change_cotangent,
    )
    outs = pl.pallas_call(
        functools.partial(kernel, nres, nsub),
        out_shape=shapes,
        in_specs=[anywhere] * 8,
        out_specs=(anywhere,) * 6,
        scratch_shapes=[pltpu.VMEM(a.shape, a.dtype) for a in operands + shapes] + [
            pltpu.VMEM((128, 128), bf16),
            pltpu.VMEM((128, 128), bf16),
            pltpu.VMEM((16, 384), bf16),
            pltpu.VMEM((2, nres // 4, 2, 16, 384), bf16),
            pltpu.VMEM((128, 4096), bf16),
            pltpu.VMEM((1024, 128), f32),
            pltpu.VMEM((2, 256, 2048), bf16),
            pltpu.VMEM((128, 2048), bf16),
            pltpu.VMEM((2, 128, 4096), bf16),
            pltpu.VMEM((nres, 16, 256), bf16),
            pltpu.VMEM((nres, 16, 256), bf16),
            pltpu.VMEM((8, n * 4, 128), bf16),
            pltpu.VMEM((8, n * 4, 128), bf16),
            pltpu.VMEM((8, n * 4, 128), bf16),
            pltpu.VMEM((n // 8, 32, 128), bf16),
            pltpu.VMEM((n // 8, 32, 128), bf16),
            pltpu.VMEM((32, 128), bf16),
            pltpu.VMEM((128, 128), bf16),
            pltpu.VMEM((128, 128), bf16),
            pltpu.VMEM((48, 128), bf16),
            pltpu.VMEM((8, 48, 128), bf16),
            pltpu.VMEM((48, 128), bf16),
            pltpu.VMEM((n // 8, 48, 128), bf16),
            pltpu.VMEM((128, 64), f32),
            dma((8,)), dma((6,)),
            dma((nres,)), dma((nres,)),
            dma((nres,)), dma((nres,)),
            dma((8,)), dma((8,)),
            dma((8,)), dma((8,)),
            dma((8,)), dma((8,)),
            dma((2,)), dma((2,)),
            dma((n // 8,)), dma((n // 8,)),
            dma((n // 8,)), dma((n // 8,)),
            dma((n // 8,)), dma((n // 8,)),
        ],
        compiler_params=pltpu.CompilerParams(
            collective_id=0, has_side_effects=True, vmem_limit_bytes=60 * 1024 * 1024
        ),
    )(*operands)
    outs = pl.pallas_call(
        hand_over,
        out_shape=shapes,
        in_specs=[anywhere] * 6,
        out_specs=(anywhere,) * 6,
        scratch_shapes=[pltpu.VMEM(a.shape, a.dtype) for a in shapes] + [dma((6,)), dma((6,))],
        compiler_params=pltpu.CompilerParams(vmem_limit_bytes=60 * 1024 * 1024),
    )(*outs)
    return (outs[0], outs[1], outs[2].T, outs[3].T, outs[4], outs[5].reshape(128))


def body(
    sequence_embedding,
    sequence_present_flags,
    position_couple_flags,
    first_factor_matrix,
    second_factor_matrix,
    final_linear_matrix,
    final_offset_vector,
    couple_change_cotangent,
):
    highest = lax.Precision.HIGHEST
    precise_scalar = jnp.float32
    hidden = first_factor_matrix.shape[1]
    pair_width = final_linear_matrix.shape[1]
    position_span = sequence_embedding.shape[1]
    col_width = couple_change_cotangent.shape[1]
    col_start = lax.axis_index("sub") * col_width
    present_count_items = sequence_embedding.astype(precise_scalar)
    centred = present_count_items - jnp.mean(present_count_items, axis=-1, keepdims=True)
    variance = jnp.mean(centred * centred, axis=-1, keepdims=True)
    reciprocal_deviation = lax.rsqrt(variance + 1e-05)
    normalized_input = centred * reciprocal_deviation
    layer_scaled_half = normalized_input.astype(jnp.bfloat16)
    row_presence_mask = sequence_present_flags.astype(precise_scalar)[:, None, :]
    first_factor_features = jnp.einsum(
        "sim,mc->sci", layer_scaled_half, first_factor_matrix, preferred_element_type=precise_scalar
    )
    second_factor_features = jnp.einsum(
        "sim,mc->sci",
        layer_scaled_half,
        second_factor_matrix,
        preferred_element_type=precise_scalar,
    )
    feat_a = (first_factor_features * row_presence_mask).astype(jnp.bfloat16)
    feat_b = (second_factor_features * row_presence_mask).astype(jnp.bfloat16)
    mask16 = row_presence_mask.astype(jnp.bfloat16)
    all_a, all_b, all_mask = (
        lax.all_gather(feat_a, "sub", axis=0, tiled=True),
        lax.all_gather(feat_b, "sub", axis=0, tiled=True),
        lax.all_gather(mask16, "sub", axis=0, tiled=True),
    )
    wide_b, wide_mask = (
        lax.all_gather(all_b, "res", axis=2, tiled=True),
        lax.all_gather(all_mask, "res", axis=2, tiled=True),
    )
    col_b = lax.dynamic_slice_in_dim(wide_b, col_start, col_width, 2)
    col_mask = lax.dynamic_slice_in_dim(wide_mask, col_start, col_width, 2)
    pair_count = jnp.einsum(
        "sxi,sxj->ij", all_mask, col_mask, preferred_element_type=precise_scalar
    )
    divisor = jnp.maximum(pair_count, 1.0)[:, :, None]
    out_cube = final_linear_matrix.reshape(hidden, hidden, pair_width)
    tmix = jnp.einsum(
        "sci,cde->side", all_a, out_cube, preferred_element_type=precise_scalar
    ).astype(jnp.bfloat16)
    zsum = jnp.einsum("side,sdj->ije", tmix, col_b, preferred_element_type=precise_scalar)
    pmask = position_couple_flags.astype(precise_scalar)[:, :, None]
    pair_delta_output = (pmask * (zsum + final_offset_vector) / divisor).astype(jnp.bfloat16)
    gscaled32 = couple_change_cotangent * pmask / divisor
    bias_part = jnp.sum(gscaled32, axis=(0, 1))
    gscaled = gscaled32.astype(jnp.bfloat16)
    dtmix = jnp.einsum("ije,sdj->side", gscaled, col_b, preferred_element_type=precise_scalar)
    db_part = jnp.einsum("ije,side->sdj", gscaled, tmix, preferred_element_type=precise_scalar)
    cube_f32 = out_cube.astype(precise_scalar)
    da_part = jnp.einsum("side,cde->sci", dtmix, cube_f32, precision=highest)
    out_part = jnp.einsum("sci,side->cde", all_a.astype(precise_scalar), dtmix, precision=highest)
    placed = jnp.zeros((db_part.shape[0], hidden, wide_b.shape[2]), precise_scalar)
    placed = lax.dynamic_update_slice_in_dim(placed, db_part, col_start, 2)
    res_totals = lax.psum_scatter(placed, "res", scatter_dimension=2, tiled=True)
    da_rows, db_rows = (
        lax.psum_scatter(da_part, "sub", scatter_dimension=0, tiled=True),
        lax.psum_scatter(res_totals, "sub", scatter_dimension=0, tiled=True),
    )
    dfeat_a = da_rows * row_presence_mask
    dfeat_b = db_rows * row_presence_mask
    normed_f = layer_scaled_half.astype(precise_scalar)
    wa_part = jnp.einsum("sim,sci->mc", normed_f, dfeat_a, precision=highest)
    wb_part = jnp.einsum("sim,sci->mc", normed_f, dfeat_b, precision=highest)
    totals = lax.psum((out_part, bias_part, wa_part, wb_part), ("res", "sub"))
    inv_res = 1.0 / (position_span * lax.axis_size("res"))
    output_weight_gradient = totals[0].reshape(hidden * hidden, pair_width) * inv_res
    output_bias_gradient = totals[1] * inv_res
    left_weight_gradient = totals[2] * inv_res
    right_weight_gradient = totals[3] * inv_res
    normalized_gradient = jnp.einsum(
        "sci,mc->sim", dfeat_a, first_factor_matrix.astype(precise_scalar), precision=highest
    )
    normalized_gradient = normalized_gradient + jnp.einsum(
        "sci,mc->sim", dfeat_b, second_factor_matrix.astype(precise_scalar), precision=highest
    )
    alignment_gradient = reciprocal_deviation * (
        normalized_gradient
        - jnp.mean(normalized_gradient, axis=-1, keepdims=True)
        - normalized_input
        * jnp.mean(normalized_gradient * normalized_input, axis=-1, keepdims=True)
    )
    return (
        pair_delta_output,
        alignment_gradient,
        left_weight_gradient,
        right_weight_gradient,
        output_weight_gradient,
        output_bias_gradient,
    )


def solution(mesh):
    in_specs = (
        P("sub", ("groups", "res"), None),
        P("sub", ("groups", "res")),
        P(("groups", "res"), "sub"),
        P(),
        P(),
        P(),
        P(),
        P(("groups", "res"), "sub", None),
    )
    out_specs = (
        P(("groups", "res"), "sub", None),
        P("sub", ("groups", "res"), None),
        P("groups", None),
        P("groups", None),
        P("groups", None),
        P("groups"),
    )
    nres, nsub = mesh.shape["res"], mesh.shape["sub"]
    chosen = functools.partial(fused, nres, nsub) if (nres, nsub) == (16, 2) else body
    return jax.shard_map(chosen, mesh=mesh, in_specs=in_specs, out_specs=out_specs, check_vma=False)
```
